512 devices in a mesh: dp: 4 (over y_lo), seq: 16 (over z, y_hi), head: 8 (over x, core).
Axes of the slice: x: 4, y: 8 (y_hi: 2, y_lo: 4; y = y_hi * 4 + y_lo), z: 8, core: 2. Of those that a mesh axis runs over, the one named last changes fastest.
Arguments:
- spatial_query: bfloat16 [4, 16, 256, 2048], P('dp', 'seq', None, 'head'), may hold values from -10 to 10
- spatial_key: bfloat16 [4, 16, 256, 2048], P('dp', 'seq', None, 'head'), may hold values from -10 to 10
- spatial_value: bfloat16 [4, 16, 256, 2048], P('dp', 'seq', None, 'head'), may hold values from -6 to 6
- spatial_mask: int32 [4, 16, 16, 2, 2], P('dp', 'seq', 'head'), may hold values from 0 to 1, as said below
- temporal_query: bfloat16 [4, 16, 256, 2048], P('dp', 'seq', None, 'head'), may hold values from -10 to 10
- temporal_key: bfloat16 [4, 16, 256, 2048], P('dp', 'seq', None, 'head'), may hold values from -10 to 10
- temporal_value: bfloat16 [4, 16, 256, 2048], P('dp', 'seq', None, 'head'), may hold values from -6 to 6
- spatial_proj: bfloat16 [2048, 3072], P('head', 'seq'), may hold values from -0.125 to 0.125
- temporal_proj: bfloat16 [2048, 3072], P('head', 'seq'), may hold values from -0.125 to 0.125
- cotangent: bfloat16 [4, 16, 256, 3072], P('dp', 'seq', None, 'head'), may hold values from -6 to 6
Outputs:
- block_update: bfloat16 [4, 16, 256, 3072], P('dp', 'seq', None, 'head')
- grad_spatial_query: bfloat16 [4, 16, 256, 2048], P('dp', 'seq', None, 'head')
- grad_spatial_key: bfloat16 [4, 16, 256, 2048], P('dp', 'seq', None, 'head')
- grad_spatial_value: bfloat16 [4, 16, 256, 2048], P('dp', 'seq', None, 'head')
- grad_temporal_query: bfloat16 [4, 16, 256, 2048], P('dp', 'seq', None, 'head')
- grad_temporal_key: bfloat16 [4, 16, 256, 2048], P('dp', 'seq', None, 'head')
- grad_temporal_value: bfloat16 [4, 16, 256, 2048], P('dp', 'seq', None, 'head')
- grad_spatial_proj: float32 [2048, 3072], P('head', 'seq')
- grad_temporal_proj: float32 [2048, 3072], P('head', 'seq')
The draws below stay inside these ranges and needn't reach their ends.
Inputs may be any that keep to these rules, and one draw needn't show every extreme that they name: `spatial_mask`: every tile on the diagonal (a query tile with its own key tile) is 1.
All inputs are finite; a program needn't handle non-finite values.
Results may differ from the reference program's by a relative error of at most 0.019.
Values may be sent and summed in bfloat16 or wider, within the bound.
A program may use at most 64 MiB of HBM per device.

```python
import math
import jax
import jax.numpy as jnp
from jax import lax

D = 3072
HEADS = 16
HDIM = 128
FRAMES = 16
FTOK = 256
CLIP_DEV = 1
CLIPS = 4
HD = 2048
NB = 2


def draw_spatial_query(key, part):
    own_key = jax.random.fold_in(key, 1)
    shape = (CLIPS, FRAMES, FTOK, HEADS, HDIM)
    values = jnp.clip(1.4 * jax.random.normal(own_key, shape, jnp.float32), -5.6, 5.6)
    return values.reshape(CLIPS, FRAMES, FTOK, HEADS * HDIM).astype(jnp.bfloat16)


def draw_spatial_key(key, part):
    own_key = jax.random.fold_in(key, 2)
    shape = (CLIPS, FRAMES, FTOK, HEADS, HDIM)
    values = jnp.clip(1.4 * jax.random.normal(own_key, shape, jnp.float32), -5.6, 5.6)
    return values.reshape(CLIPS, FRAMES, FTOK, HEADS * HDIM).astype(jnp.bfloat16)


def draw_temporal_query(key, part):
    own_key = jax.random.fold_in(key, 3)
    shape = (CLIPS, FRAMES, FTOK, HEADS, HDIM)
    values = jnp.clip(1.4 * jax.random.normal(own_key, shape, jnp.float32), -5.6, 5.6)
    return values.reshape(CLIPS, FRAMES, FTOK, HEADS * HDIM).astype(jnp.bfloat16)


def draw_temporal_key(key, part):
    own_key = jax.random.fold_in(key, 4)
    shape = (CLIPS, FRAMES, FTOK, HEADS, HDIM)
    values = jnp.clip(1.4 * jax.random.normal(own_key, shape, jnp.float32), -5.6, 5.6)
    return values.reshape(CLIPS, FRAMES, FTOK, HEADS * HDIM).astype(jnp.bfloat16)


def draw_spatial_mask(key, part):
    key = jax.random.fold_in(key, 7)
    shape = (CLIPS, FRAMES, HEADS, NB, NB)
    random_bits = jax.random.randint(key, shape, 0, 2)
    diagonal = (lax.broadcasted_iota(jnp.int32, shape, 3) == lax.broadcasted_iota(jnp.int32, shape, 4)).astype(jnp.int32)
    return jnp.maximum(random_bits, diagonal)


def shard_levels(key, shape, shards, least, high):
    loudness, own = 1.0, jax.random.fold_in(key, 6)
    for position, blocks in shards:
        steps = jnp.exp(jax.random.uniform(jax.random.fold_in(own, position), (blocks,), jnp.float32, least / len(shards), high / len(shards)))
        loudness = loudness * jnp.repeat(steps, shape[position] // blocks).reshape([-1 if axis == position else 1 for axis in range(len(shape))])
    return loudness


def centred(stream_key, extent, width, most, pieces=(), kind=jnp.bfloat16):
    array = width * jax.random.normal(stream_key, extent, jnp.float32)
    if pieces:
        array = array * shard_levels(stream_key, extent, pieces, -0.22, 0.18)
    return jnp.clip(array, -most, most).astype(kind)


def setup_inputs(seed: int = 0) -> dict:
    seeds = jax.random.split(jax.random.key(seed), 11)
    spatial_query = draw_spatial_query(jax.random.fold_in(seeds[10], 71), 0)
    spatial_key = draw_spatial_key(jax.random.fold_in(seeds[10], 71), 0)
    spatial_value = centred(seeds[2], (CLIPS, FRAMES, FTOK, HD), 1.0, 6.0, ((0, 4), (1, 16), (3, 8)))
    spatial_mask = draw_spatial_mask(jax.random.fold_in(seeds[10], 71), 0)
    temporal_query = draw_temporal_query(jax.random.fold_in(seeds[10], 71), 0)
    temporal_key = draw_temporal_key(jax.random.fold_in(seeds[10], 71), 0)
    temporal_value = centred(seeds[6], (CLIPS, FRAMES, FTOK, HD), 1.0, 6.0, ((0, 4), (1, 16), (3, 8)))
    spatial_proj = centred(seeds[7], (HD, D), HD ** -0.5, 0.125, ((0, 8), (1, 16)))
    temporal_proj = centred(seeds[8], (HD, D), HD ** -0.5, 0.125, ((0, 8), (1, 16)))
    cotangent = centred(seeds[9], (CLIPS, FRAMES, FTOK, D), 1.0, 6.0, ((0, 4), (1, 16), (3, 8)))
    return {"spatial_query": spatial_query, "spatial_key": spatial_key, "spatial_value": spatial_value, "spatial_mask": spatial_mask, "temporal_query": temporal_query, "temporal_key": temporal_key, "temporal_value": temporal_value, "spatial_proj": spatial_proj, "temporal_proj": temporal_proj, "cotangent": cotangent}


def spatial_forward(query, keys, values, mask, score_scale):
    frame_count, tokens, head_count, head_dim = query.shape
    blocks = mask.shape[-1]
    tile_size = tokens // blocks
    scores = jnp.einsum('fqhd,fkhd->fhqk', query.astype(jnp.float32), keys.astype(jnp.float32)) * score_scale
    scores = scores.reshape(frame_count, head_count, blocks, tile_size, blocks, tile_size)
    allowed = mask[:, :, :, None, :, None] > 0
    scores = jnp.where(allowed, scores, -jnp.inf).reshape(frame_count, head_count, tokens, tokens)
    shares = jax.nn.softmax(scores, axis=-1)
    weights = shares.astype(jnp.bfloat16)
    attended = jnp.einsum('fhqk,fkhd->fqhd', weights.astype(jnp.float32), values.astype(jnp.float32)).astype(jnp.bfloat16)
    return (shares, weights, attended)

def spatial_backward(query, keys, values, shares, weights, grad_att, score_scale):
    grad_shares = jnp.einsum('fqhd,fkhd->fhqk', grad_att.astype(jnp.float32), values.astype(jnp.float32))
    centre = lax.optimization_barrier(jnp.sum(shares * grad_shares, axis=-1, keepdims=True))
    grad_scores = (shares * (grad_shares - centre)).astype(jnp.bfloat16).astype(jnp.float32)
    grad_query = (jnp.einsum('fhqk,fkhd->fqhd', grad_scores, keys.astype(jnp.float32)) * score_scale).astype(jnp.bfloat16)
    grad_keys = (jnp.einsum('fhqk,fqhd->fkhd', grad_scores, query.astype(jnp.float32)) * score_scale).astype(jnp.bfloat16)
    grad_values = jnp.einsum('fhqk,fqhd->fkhd', weights.astype(jnp.float32), grad_att.astype(jnp.float32)).astype(jnp.bfloat16)
    return (grad_query, grad_keys, grad_values)

def temporal_forward(query, keys, values, score_scale):
    scores = jnp.einsum('fthd,gthd->thfg', query.astype(jnp.float32), keys.astype(jnp.float32)) * score_scale
    shares = jax.nn.softmax(scores, axis=-1)
    weights = shares.astype(jnp.bfloat16)
    attended = jnp.einsum('thfg,gthd->fthd', weights.astype(jnp.float32), values.astype(jnp.float32)).astype(jnp.bfloat16)
    return (shares, weights, attended)

def temporal_backward(query, keys, values, shares, weights, grad_att, score_scale):
    grad_shares = jnp.einsum('fthd,gthd->thfg', grad_att.astype(jnp.float32), values.astype(jnp.float32))
    centre = lax.optimization_barrier(jnp.sum(shares * grad_shares, axis=-1, keepdims=True))
    grad_scores = (shares * (grad_shares - centre)).astype(jnp.bfloat16).astype(jnp.float32)
    grad_query = (jnp.einsum('thfg,gthd->fthd', grad_scores, keys.astype(jnp.float32)) * score_scale).astype(jnp.bfloat16)
    grad_keys = (jnp.einsum('thfg,fthd->gthd', grad_scores, query.astype(jnp.float32)) * score_scale).astype(jnp.bfloat16)
    grad_values = jnp.einsum('thfg,fthd->gthd', weights.astype(jnp.float32), grad_att.astype(jnp.float32)).astype(jnp.bfloat16)
    return (grad_query, grad_keys, grad_values)

def reference(spatial_query, spatial_key, spatial_value, spatial_mask, temporal_query, temporal_key, temporal_value, spatial_proj, temporal_proj, cotangent):
    split_shape = (FRAMES, FTOK, HEADS, HDIM)
    flat_shape = (FRAMES, FTOK, HEADS * HDIM)
    row_count = FRAMES * FTOK
    score_scale = 1.0 / math.sqrt(HDIM)

    def one_clip(items):
        s_query, s_key, s_value, s_mask, t_query, t_key, t_value, cot = items
        s_query = s_query.reshape(split_shape)
        s_key = s_key.reshape(split_shape)
        s_value = s_value.reshape(split_shape)
        t_query = t_query.reshape(split_shape)
        t_key = t_key.reshape(split_shape)
        t_value = t_value.reshape(split_shape)
        s_shares, s_weights, s_attended = spatial_forward(s_query, s_key, s_value, s_mask, score_scale)
        t_shares, t_weights, t_attended = temporal_forward(t_query, t_key, t_value, score_scale)
        spatial_rows = s_attended.reshape(row_count, HEADS * HDIM)
        temporal_rows = t_attended.reshape(row_count, HEADS * HDIM)
        update = jnp.dot(spatial_rows, spatial_proj, preferred_element_type=jnp.float32)
        update = update + jnp.dot(temporal_rows, temporal_proj, preferred_element_type=jnp.float32)
        update = update.astype(jnp.bfloat16).reshape(FRAMES, FTOK, D)
        cot_rows = cot.reshape(row_count, D)
        grad_s_att = jnp.dot(cot_rows, spatial_proj.T, preferred_element_type=jnp.float32).astype(jnp.bfloat16)
        grad_t_att = jnp.dot(cot_rows, temporal_proj.T, preferred_element_type=jnp.float32).astype(jnp.bfloat16)
        spatial_wgrad = jnp.dot(spatial_rows.T, cot_rows, preferred_element_type=jnp.float32)
        temporal_wgrad = jnp.dot(temporal_rows.T, cot_rows, preferred_element_type=jnp.float32)
        sq_grad, sk_grad, sv_grad = spatial_backward(s_query, s_key, s_value, s_shares, s_weights, grad_s_att.reshape(split_shape), score_scale)
        tq_grad, tk_grad, tv_grad = temporal_backward(t_query, t_key, t_value, t_shares, t_weights, grad_t_att.reshape(split_shape), score_scale)
        return (update, sq_grad.reshape(flat_shape), sk_grad.reshape(flat_shape), sv_grad.reshape(flat_shape), tq_grad.reshape(flat_shape), tk_grad.reshape(flat_shape), tv_grad.reshape(flat_shape), spatial_wgrad, temporal_wgrad)
    results = lax.map(one_clip, (spatial_query, spatial_key, spatial_value, spatial_mask, temporal_query, temporal_key, temporal_value, cotangent))
    replicas = CLIPS // CLIP_DEV
    grad_spatial_proj = lax.optimization_barrier(jnp.sum(results[7], axis=0)) / replicas
    grad_temporal_proj = lax.optimization_barrier(jnp.sum(results[8], axis=0)) / replicas
    return (results[0], results[1], results[2], results[3], results[4], results[5], results[6], grad_spatial_proj, grad_temporal_proj)
```

```python
import functools
import math

import jax
import jax.numpy as jnp
from jax import lax
from jax.experimental import pallas as pl
from jax.experimental.pallas import tpu as pltpu
from jax.sharding import PartitionSpec as P

MESH = pl.DeviceIdType.MESH
BF16 = jnp.bfloat16
F32 = jnp.float32
NEG = -1e30


def dot(a, b):
    return lax.dot_general(a, b, (((1,), (0,)), ((), ())), preferred_element_type=F32)


def dot_nt(a, b):
    return lax.dot_general(a, b, (((1,), (1,)), ((), ())), preferred_element_type=F32)


def dot_tn(a, b):
    return lax.dot_general(a, b, (((0,), (0,)), ((), ())), preferred_element_type=F32)


def wait_for(view, sem):
    pltpu.make_async_copy(view, view, sem).wait()


def kernel(
    dims,
    sq, sk, sv, mask, tq, tk, tv, sp, tp, cot,
    upd, gsq, gsk, gsv, gtq, gtk, gtv, gsp, gtp,
    wts, wtt, wtmp, cotb, tqb, tkb, tvb,
    s_shares, t_shares, s_att, t_att, t_att_tok, gs_acc, gt_acc, g_t, g_tok, q_g, k_g, v_g,
    ps, pt, rs_s, rs_t, rs_s_half, rs_t_half, sec_s, sec_t, fin,
    u_out, u_in, u_keep, u_send, u_recv,
    sems,
):
    NDP, NSEQ, NHEAD, HL, HDIM, Q = dims
    Z, Y, X = NSEQ // 2, NDP * 2, NHEAD // 2
    TOK, LW = sq.shape
    TB = TOK // NSEQ
    DH = cot.shape[1]
    scale = 1.0 / math.sqrt(HDIM)

    dp = lax.axis_index("dp")
    seq = lax.axis_index("seq")
    head = lax.axis_index("head")
    z, yh = seq // 2, lax.rem(seq, 2)
    y = yh * NDP + dp
    x, core = head // 2, lax.rem(head, 2)

    def at_y(place):
        return {"dp": lax.rem(place, NDP), "seq": z * 2 + place // NDP}

    def at_z(place):
        return {"seq": place * 2 + yh}

    def at_x(place):
        return {"head": place * 2 + core}

    sibling = {"head": x * 2 + 1 - core}
    counter = iter(range(1000))

    def sem():
        return sems.at[next(counter)]

    def send(src, dst, send_sem, recv_sem, to):
        pltpu.make_async_remote_copy(
            src_ref=src, dst_ref=dst, send_sem=send_sem, recv_sem=recv_sem,
            device_id=to, device_id_type=MESH,
        ).start()

    barrier = pltpu.get_barrier_semaphore()

    def greet(to):
        pl.semaphore_signal(barrier, inc=1, device_id=to, device_id_type=MESH)

    @pl.loop(1, NSEQ)
    def _(i):
        greet({"seq": lax.rem(seq + i, NSEQ)})

    @pl.loop(1, NDP)
    def _(i):
        other = lax.rem(dp + i, NDP)
        greet({"dp": other, "seq": z * 2})
        greet({"dp": other, "seq": z * 2 + 1})

    @pl.loop(1, X)
    def _(i):
        greet(at_x(lax.rem(x + i, X)))

    greet(sibling)

    DS = sp.shape[1]
    eye = (
        lax.broadcasted_iota(jnp.int32, (DS, DS), 0) == lax.broadcasted_iota(jnp.int32, (DS, DS), 1)
    ).astype(F32).astype(BF16)
    wts[z, pl.ds(yh * NDP, NDP)] = dot_nt(eye, sp[...]).astype(BF16).reshape(NDP, Q, LW)
    wtmp[...] = dot_nt(eye, tp[...]).astype(BF16).reshape(NDP, Q, LW)
    wtt[y, z] = wtmp[dp]

    pl.semaphore_wait(barrier, NSEQ - 1 + 2 * (NDP - 1) + X)

    def all_to_all(src, dst, send_sem, recv_sem):
        mine = pl.ds(pl.multiple_of(seq * TB, TB), TB)

        @pl.loop(1, NSEQ)
        def _(i):
            other = lax.rem(seq + i, NSEQ)
            send(
                src.at[pl.ds(pl.multiple_of(other * TB, TB), TB)], dst.at[mine],
                send_sem, recv_sem, {"seq": other},
            )

    def rest(ref):
        return ref.at[pl.ds(0, (NSEQ - 1) * TB)]

    mine = pl.ds(pl.multiple_of(seq * TB, TB), TB)
    qkv = ((tq, tqb), (tk, tkb), (tv, tvb))
    qkv_s, qkv_r, qkv_l = [sem() for _ in qkv], [sem() for _ in qkv], [sem() for _ in qkv]
    for (src, dst), s, r, l in zip(qkv, qkv_s, qkv_r, qkv_l):
        all_to_all(src, dst, s, r)
        pltpu.make_async_copy(src.at[mine], dst.at[mine], l).start()

    mir_s, mir_r = sem(), sem()
    own_s = wts.at[z, pl.ds(yh * NDP, NDP)]
    send(own_s, own_s, mir_s, mir_r, {"dp": NDP - 1 - dp, "seq": z * 2 + 1 - yh})

    zq_s, zq_r = sem(), sem()

    @pl.loop(1, Z)
    def _(i):
        send(wtt.at[y, z], wtt.at[y, z], zq_s, zq_r, at_z(lax.rem(z + i, Z)))

    cot_l, cot_s = sem(), [sem() for _ in range(X)]
    cot_r = [sem() for _ in range(X - 1)]
    cot_sib = sem()
    pltpu.make_async_copy(cot, cotb.at[head], cot_l).start()
    for i in range(1, X):
        send(cot, cotb.at[head], cot_s[i - 1], cot_r[i - 1], at_x(lax.rem(x + i, X)))
    send(cot, cotb.at[head], cot_s[X - 1], cot_sib, sibling)

    def heads(ref, h):
        return ref[:, h * HDIM : (h + 1) * HDIM]

    def forward(h, q, k, v, bias, shares):
        scores = dot_nt(heads(q, h), heads(k, h)) * scale + bias
        e = jnp.exp(scores - jnp.max(scores, axis=-1, keepdims=True))
        part = e * (1.0 / jnp.sum(e, axis=-1, keepdims=True))
        shares[h] = part
        return dot(part.astype(BF16), heads(v, h)).astype(BF16)

    def backward(h, q, k, v, g, shares):
        share = shares[h]
        weight = share.astype(BF16)
        grad = heads(g, h)
        grad_shares = dot_nt(grad, heads(v, h))
        centre = jnp.sum(share * grad_shares, axis=-1, keepdims=True)
        grad_scores = (share * (grad_shares - centre)).astype(BF16)
        dq = (dot(grad_scores, heads(k, h)) * scale).astype(BF16)
        dk = (dot_tn(grad_scores, heads(q, h)) * scale).astype(BF16)
        dv = dot_tn(weight, grad).astype(BF16)
        return dq, dk, dv

    NB = mask.shape[-1]
    tile = TOK // NB
    rows = lax.broadcasted_iota(jnp.int32, (TOK, TOK), 0)
    cols = lax.broadcasted_iota(jnp.int32, (TOK, TOK), 1)
    for h in range(HL):
        bias = jnp.zeros((TOK, TOK), F32)
        for a in range(NB):
            for b in range(NB):
                value = (mask[0, 0, h, a, b].astype(F32) - 1.0) * -NEG
                inside = jnp.logical_and(rows // tile == a, cols // tile == b)
                bias = jnp.where(inside, value, bias)
        s_att[:, h * HDIM : (h + 1) * HDIM] = forward(h, sq, sk, sv, bias, s_shares)

    def ring_ids(n, me, where):
        return where(lax.rem(me + 1, n)), where(lax.rem(me + n - 1, n))

    class Gather:
        def __init__(self, buf, n, me, where):
            self.buf, self.n, self.me = buf, n, me
            self.right, self.left = ring_ids(n, me, where)
            self.half = n // 2
            self.s = [[sem() for _ in range(self.half)] for _ in range(2)]
            self.r = [[sem() for _ in range(self.half)] for _ in range(2)]

        def view(self, way, step, k):
            sign = -1 if way == 0 else 1
            chunk = lax.rem(self.me + sign * k + self.n, self.n)
            if step < self.half:
                return self.buf.at[chunk]
            size = self.buf.shape[1] // 2
            return self.buf.at[chunk, pl.ds(way * size, size)]

        def start(self, step):
            for way, to in ((0, self.right), (1, self.left)):
                if step > 1:
                    wait_for(self.view(way, step - 1, step - 1), self.r[way][step - 2])
                v = self.view(way, step, step - 1)
                send(v, v, self.s[way][step - 1], self.r[way][step - 1], to)

        def finish(self):
            for way in range(2):
                wait_for(self.view(way, self.half, self.half), self.r[way][self.half - 1])

        def drain(self):
            for way in range(2):
                for step in range(1, self.half + 1):
                    wait_for(self.view(way, step, step - 1), self.s[way][step - 1])

    class Scatter:
        def __init__(self, buf, arrive, arrive_half, n, me, where):
            self.buf, self.n, self.me = buf, n, me
            self.arrive, self.arrive_half = arrive, arrive_half
            self.right, self.left = ring_ids(n, me, where)
            self.half = n // 2
            self.s = [[sem() for _ in range(self.half)] for _ in range(2)]
            self.r = [[sem() for _ in range(self.half)] for _ in range(2)]

        def dest(self, way, step):
            sign = 1 if way == 0 else -1
            return lax.rem(self.me + sign * (self.half + 1 - step) + self.n, self.n)

        def source(self, way, step):
            if step > 1:
                return self.buf.at[self.dest(way, step)]
            size = self.buf.shape[1] // 2
            return self.buf.at[self.dest(way, 1), pl.ds(way * size, size)]

        def landing(self, way, step):
            return self.arrive_half.at[way] if step == 1 else self.arrive.at[way, step - 2]

        def start(self, step):
            for way, to in ((0, self.right), (1, self.left)):
                if step > 1:
                    landed = self.landing(way, step - 1)
                    wait_for(landed, self.r[way][step - 2])
                    d = self.dest(way, step)
                    size = self.buf.shape[1] // 2
                    where = pl.ds(way * size, size) if step == 2 else pl.ds(0, 2 * size)
                    total = self.buf[d, where].astype(F32) + landed[...].astype(F32)
                    self.buf[d, where] = total.astype(BF16)
                send(
                    self.source(way, step), self.landing(way, step),
                    self.s[way][step - 1], self.r[way][step - 1], to,
                )

        def finish(self):
            total = self.buf[self.me].astype(F32)
            for way in range(2):
                landed = self.landing(way, self.half)
                wait_for(landed, self.r[way][self.half - 1])
                total = total + landed[...].astype(F32)
            self.buf[self.me] = total.astype(BF16)

        def drain(self):
            for way in range(2):
                for step in range(1, self.half + 1):
                    wait_for(self.source(way, step), self.s[way][step - 1])

    wz = Gather(wts, Z, z, at_z)
    wy = Gather(wtt, Y, y, at_y)
    wait_for(own_s, mir_r)
    wz.start(1)
    wait_for(wtt.at[y, pl.ds(0, Z - 1)], zq_r)
    wy.start(1)

    for (src, dst), r, l in zip(qkv, qkv_r, qkv_l):
        wait_for(rest(dst), r)
        wait_for(dst.at[mine], l)
    same = jnp.where(lax.rem(rows, TB) == lax.rem(cols, TB), 0.0, NEG).astype(F32)
    for h in range(HL):
        t_att_tok[:, h * HDIM : (h + 1) * HDIM] = forward(h, tqb, tkb, tvb, same, t_shares)
    ta_s, ta_r = sem(), sem()
    all_to_all(t_att_tok, t_att, ta_s, ta_r)
    t_att[mine] = t_att_tok[mine]

    fwd_s, fwd_r = [sem() for _ in range(X - 1)], [sem() for _ in range(X - 1)]
    for i in range(1, X):
        slot = cotb.at[lax.rem(x + X - i, X) * 2 + core]
        wait_for(slot, cot_r[i - 1])
        send(slot, slot, fwd_s[i - 1], fwd_r[i - 1], sibling)

    wz.start(2)
    wy.start(2)
    wait_for(cotb.at[head], cot_l)
    wait_for(cotb.at[head], cot_sib)
    for i in range(1, X):
        wait_for(cotb.at[head], fwd_r[i - 1])

    @pl.loop(0, Z)
    def _(b):
        ps[b] = dot_tn(cotb[b], s_att[...]).astype(BF16).reshape(Y, Q, LW)

    wz.start(3) if wz.half >= 3 else None
    wy.start(3) if wy.half >= 3 else None
    wait_for(rest(t_att), ta_r)

    @pl.loop(0, Z)
    def _(b):
        pt[:, pl.ds(b, 1)] = dot_tn(cotb[b], t_att[...]).astype(BF16).reshape(Y, 1, Q, LW)

    for step in range(4, wz.half + 1):
        wz.start(step)
        wy.start(step)
    wz.finish()
    wy.finish()

    gs_acc[...] = jnp.zeros_like(gs_acc)
    gt_acc[...] = jnp.zeros_like(gt_acc)

    def block_t(b):
        return wtt[:, pl.ds(b, 1)].reshape(DH, LW)

    def block_s(b):
        return wts[b].reshape(DH, LW)

    @pl.loop(0, Z)
    def _(b):
        gt_acc[...] += dot(cotb[b], block_t(b))
        gs_acc[...] += dot(cotb[b], block_s(b))

    g_t[...] = gt_acc[...].astype(BF16)
    gt_s, gt_r = sem(), sem()
    all_to_all(g_t, g_tok, gt_s, gt_r)
    g_tok[mine] = g_t[mine]

    rz = Scatter(ps, rs_s, rs_s_half, Z, z, at_z)
    ry = Scatter(pt, rs_t, rs_t_half, Y, y, at_y)
    rz.start(1)
    ry.start(1)

    def update(b):
        return dot_nt(s_att[...], block_s(b)) + dot_nt(t_att[...], block_t(b))

    us_s, us_r = sem(), sem()

    @pl.loop(0, X)
    def _(i):
        u_out[i] = update(i * 2 + 1 - core).astype(BF16)
        send(u_out.at[i], u_in.at[i], us_s, us_r, sibling)

    rz.start(2)
    ry.start(2)

    @pl.loop(0, X)
    def _(i):
        u_keep[i] = update(i * 2 + core)

    wait_for(u_in, us_r)
    ux_s, ux_r = sem(), sem()

    @pl.loop(1, X)
    def _(i):
        other = lax.rem(x + i, X)
        u_send[i - 1] = (u_keep[other] + u_in[other].astype(F32)).astype(BF16)
        send(u_send.at[i - 1], u_recv.at[i - 1], ux_s, ux_r, at_x(other))

    g_s = gs_acc[...].astype(BF16)
    for h in range(HL):
        f = slice(h * HDIM, (h + 1) * HDIM)
        gsq[:, f], gsk[:, f], gsv[:, f] = backward(h, sq, sk, sv, g_s, s_shares)

    rz.start(3) if rz.half >= 3 else None
    ry.start(3) if ry.half >= 3 else None

    wait_for(rest(g_tok), gt_r)
    for h in range(HL):
        f = slice(h * HDIM, (h + 1) * HDIM)
        q_g[:, f], k_g[:, f], v_g[:, f] = backward(h, tqb, tkb, tvb, g_tok, t_shares)
    grads = ((q_g, gtq), (k_g, gtk), (v_g, gtv))
    grads_s, grads_r = [sem() for _ in grads], [sem() for _ in grads]
    for (src, dst), s, r in zip(grads, grads_s, grads_r):
        all_to_all(src, dst, s, r)
        dst[mine] = src[mine]

    for step in range(4, rz.half + 1):
        rz.start(step)
        ry.start(step)

    wait_for(u_recv, ux_r)
    total = u_keep[x] + u_in[x].astype(F32)
    for i in range(X - 1):
        total = total + u_recv[i].astype(F32)
    upd[...] = total.astype(BF16)

    rz.finish()
    sec_ss, sec_sr = sem(), sem()

    @pl.loop(1, Y)
    def _(i):
        other = lax.rem(y + i, Y)
        send(ps.at[z, other], sec_s.at[i - 1], sec_ss, sec_sr, at_y(other))

    ry.finish()
    sec_ts, sec_tr = sem(), sem()

    @pl.loop(1, Z)
    def _(i):
        other = lax.rem(z + i, Z)
        send(pt.at[y, other], sec_t.at[i - 1], sec_ts, sec_tr, at_z(other))

    wait_for(sec_s, sec_sr)
    total = ps[z, y].astype(F32)
    for i in range(Y - 1):
        total = total + sec_s[i].astype(F32)
    fin[dp, 0] = total * (1.0 / NDP)
    wait_for(sec_t, sec_tr)
    total = pt[y, z].astype(F32)
    for i in range(Z - 1):
        total = total + sec_t[i].astype(F32)
    fin[dp, 1] = total * (1.0 / NDP)

    fin_s, fin_r = sem(), sem()

    @pl.loop(1, NDP)
    def _(i):
        send(fin.at[dp], fin.at[dp], fin_s, fin_r, {"dp": lax.rem(dp + i, NDP)})

    for (src, dst), r in zip(grads, grads_r):
        wait_for(rest(dst), r)

    for (src, dst), s in zip(qkv, qkv_s):
        wait_for(rest(dst), s)
    wait_for(own_s, mir_s)
    wait_for(wtt.at[y, pl.ds(0, Z - 1)], zq_s)
    for s in cot_s + fwd_s:
        wait_for(cotb.at[head], s)
    wz.drain()
    wy.drain()
    rz.drain()
    ry.drain()
    for s in (ta_s, gt_s):
        wait_for(rest(t_att), s)
    for s in grads_s:
        wait_for(rest(t_att), s)
    wait_for(u_in, us_s)
    wait_for(u_recv, ux_s)
    wait_for(sec_s, sec_ss)
    wait_for(sec_t, sec_ts)
    wait_for(fin.at[pl.ds(0, NDP - 1)], fin_r)
    wait_for(fin.at[pl.ds(0, NDP - 1)], fin_s)
    gsp[...] = fin[:, 0].reshape(DS, LW)
    gtp[...] = fin[:, 1].reshape(DS, LW)


def per_device(dims, *args):
    NDP, NSEQ, NHEAD = dims
    sq, sk, sv, mask, tq, tk, tv, sp, tp, cot = args
    tokens, width = sq.shape[2:]
    HL = mask.shape[2]
    HDIM = width // HL
    DS, DH = sp.shape[1], cot.shape[3]
    Z, Y, X = NSEQ // 2, NDP * 2, NHEAD // 2
    Q = DS // NDP
    flat = [a.reshape(a.shape[2:]) for a in (sq, sk, sv, tq, tk, tv, cot)]
    vmem = pl.BlockSpec(memory_space=pltpu.VMEM)
    hbm = pl.BlockSpec(memory_space=pl.ANY)
    feat = jax.ShapeDtypeStruct((tokens, width), BF16)
    proj = jax.ShapeDtypeStruct((DS, width), F32)

    def buf(*shape, dtype=BF16):
        return pltpu.VMEM(shape, dtype)

    feats = functools.partial(buf, tokens, width)
    out = pl.pallas_call(
        functools.partial(kernel, (NDP, NSEQ, NHEAD, HL, HDIM, Q)),
        out_shape=[jax.ShapeDtypeStruct((tokens, DH), BF16)] + [feat] * 6 + [proj] * 2,
        in_specs=[vmem] * 3 + [pl.BlockSpec(memory_space=pltpu.SMEM)] + [hbm] * 3 + [vmem] * 2 + [hbm],
        out_specs=[vmem] * 9,
        scratch_shapes=[
            buf(Z, Y, Q, width),
            buf(Y, Z, Q, width),
            buf(NDP, Q, width),
            buf(NHEAD, tokens, DH),
            feats(), feats(), feats(),
            buf(HL, tokens, tokens, dtype=F32),
            buf(HL, tokens, tokens, dtype=F32),
            feats(), feats(), feats(),
            feats(dtype=F32), feats(dtype=F32),
            feats(), feats(), feats(), feats(), feats(),
            buf(Z, Y, Q, width),
            buf(Y, Z, Q, width),
            buf(2, Z // 2 - 1, Y, Q, width),
            buf(2, Y // 2 - 1, Z, Q, width),
            buf(2, Y // 2, Q, width),
            buf(2, Z // 2, Q, width),
            buf(Y - 1, Q, width),
            buf(Z - 1, Q, width),
            buf(NDP, 2, Q, width, dtype=F32),
            buf(X, tokens, DH),
            buf(X, tokens, DH),
            buf(X, tokens, DH, dtype=F32),
            buf(X - 1, tokens, DH),
            buf(X - 1, tokens, DH),
            pltpu.SemaphoreType.DMA((128,)),
        ],
        compiler_params=pltpu.CompilerParams(
            collective_id=0, has_side_effects=True, vmem_limit_bytes=48 * 1024 * 1024
        ),
    )(flat[0], flat[1], flat[2], mask, flat[3], flat[4], flat[5], sp, tp, flat[6])
    return tuple(o[None, None] for o in out[:7]) + (out[7].T, out[8].T)


def solution(mesh):
    tokens = P("dp", "seq", None, "head")
    weights = P("head", "seq")
    dims = tuple(mesh.shape[a] for a in ("dp", "seq", "head"))
    return jax.shard_map(
        functools.partial(per_device, dims),
        mesh=mesh,
        in_specs=(tokens,) * 3 + (P("dp", "seq", "head", None, None),) + (tokens,) * 3 + (weights,) * 2 + (tokens,),
        out_specs=(tokens,) * 7 + (weights,) * 2,
        check_vma=False,
    )
```

```python
import functools
import math

import jax
import jax.numpy as jnp
from jax import lax
from jax.experimental import pallas as pl
from jax.experimental.pallas import tpu as pltpu
from jax.sharding import PartitionSpec as P

MESH = pl.DeviceIdType.MESH
BF16 = jnp.bfloat16
F32 = jnp.float32
NEG = -1e30
SEMS = 192


def dot(a, b):
    return lax.dot_general(a, b, (((1,), (0,)), ((), ())), preferred_element_type=F32)


def dot_nt(a, b):
    return lax.dot_general(a, b, (((1,), (1,)), ((), ())), preferred_element_type=F32)


def dot_tn(a, b):
    return lax.dot_general(a, b, (((0,), (0,)), ((), ())), preferred_element_type=F32)


def wait_for(view, sem):
    pltpu.make_async_copy(view, view, sem).wait()


def kernel(
    dims,
    sq_in, sk_in, sv_in, mask, tq, tk, tv, sp, tp, cot,
    upd, gsq, gsk, gsv, gtq, gtk, gtv, gsp, gtp,
    sq, sk, sv, wts, wtt, cotb, tqb, tkb, tvb,
    s_shares, t_shares, s_att, t_att, t_att_tok, gs_acc, gt_acc, g_t, g_tok, q_g, k_g, v_g,
    ps, pt, rs_s, rs_t, sec_s, sec_t, fin,
    u_out, u_in, u_keep, u_send, u_recv,
    sems,
):
    NDP, NSEQ, NHEAD, HL, HDIM, Q = dims
    Z, Y, X = NSEQ // 2, NDP * 2, NHEAD // 2
    TOK, LW = sq.shape
    DS = NDP * Q
    TB = TOK // NSEQ
    DH = cot.shape[1]
    scale = 1.0 / math.sqrt(HDIM)

    dp = lax.axis_index("dp")
    seq = lax.axis_index("seq")
    head = lax.axis_index("head")
    z, yh = seq // 2, lax.rem(seq, 2)
    y = yh * NDP + dp
    x, core = head // 2, lax.rem(head, 2)

    def at_y(place):
        return {"dp": lax.rem(place, NDP), "seq": z * 2 + place // NDP}

    def at_z(place):
        return {"seq": place * 2 + yh}

    def at_x(place):
        return {"head": place * 2 + core}

    sibling = {"head": x * 2 + 1 - core}
    counter = iter(range(SEMS))

    def sem(part):
        return sems.at[next(counter)]

    def local(src, dst, done):
        pltpu.make_async_copy(src, dst, done).start()

    def send(src, dst, send_sem, recv_sem, to):
        pltpu.make_async_remote_copy(
            src_ref=src, dst_ref=dst, send_sem=send_sem, recv_sem=recv_sem,
            device_id=to, device_id_type=MESH,
        ).start()

    barrier = pltpu.get_barrier_semaphore()

    def greet(to):
        pl.semaphore_signal(barrier, inc=1, device_id=to, device_id_type=MESH)

    @pl.loop(1, NSEQ)
    def _(i):
        greet({"seq": lax.rem(seq + i, NSEQ)})

    @pl.loop(1, NDP)
    def _(i):
        other = lax.rem(dp + i, NDP)
        greet({"dp": other, "seq": z * 2})
        greet({"dp": other, "seq": z * 2 + 1})

    @pl.loop(1, X)
    def _(i):
        greet(at_x(lax.rem(x + i, X)))

    greet(sibling)

    spatial = ((sq_in, sq), (sk_in, sk), (sv_in, sv))
    spatial_l = [sem("in") for _ in spatial]
    for (src, dst), l in zip(spatial, spatial_l):
        local(src, dst, l)
    own_l, cot_l = [sem("in") for _ in range(2)], sem("in")
    own_s = wts.at[z, pl.ds(yh * NDP, NDP)]
    local(sp, own_s, own_l[0])
    local(tp.at[dp], wtt.at[y, 1], own_l[1])
    local(cot, cotb.at[head], cot_l)

    pl.semaphore_wait(barrier, NSEQ - 1 + 2 * (NDP - 1) + X)

    def spatial_piece(chunk, piece):
        return wts.at[chunk, pl.ds((yh if piece == 0 else 1 - yh) * NDP, NDP)]

    def temporal_piece(chunk, piece):
        return wtt.at[chunk, pl.ds(piece * (Z // 2), Z // 2)]

    zq_s, zq_r = sem("w"), [sem("w"), sem("w")]
    for i in range(1, Z):
        slot = (1 - i) % Z
        send(tp.at[dp], wtt.at[y, slot], zq_s, zq_r[slot // (Z // 2)], at_z(lax.rem(z + i, Z)))

    mir_s, mir_r = sem("w"), sem("w")
    send(sp, own_s, mir_s, mir_r, {"dp": NDP - 1 - dp, "seq": z * 2 + 1 - yh})

    class Ring:
        def __init__(self, part, n, me, where):
            self.n, self.me = n, me
            self.to = where(lax.rem(me + 1, n)), where(lax.rem(me + n - 1, n))
            self.sems = {
                (way, piece): [(sem(part), sem(part)) for _ in range(self.hops(way, piece))]
                for way in range(2) for piece in range(2)
            }

        def hops(self, way, piece):
            return self.n // 2 if way == piece else self.n // 2 - 1

        def place(self, way, k):
            return lax.rem(self.me + (k if way == 0 else -k) + self.n, self.n)

    class Gather(Ring):
        def __init__(self, part, n, me, where, view):
            super().__init__(part, n, me, where)
            self.view = view

        def arrived(self, way, piece, j):
            wait_for(self.view(self.place(way, -j), piece), self.sems[way, piece][j - 1][1])

        def hop(self, piece, j):
            for way in range(2):
                if j <= self.hops(way, piece):
                    if j > 1:
                        self.arrived(way, piece, j - 1)
                    v = self.view(self.place(way, 1 - j), piece)
                    send(v, v, *self.sems[way, piece][j - 1], self.to[way])

        def finish(self):
            for piece in range(2):
                for way in range(2):
                    self.arrived(way, piece, self.hops(way, piece))

        def drain(self):
            for (way, piece), pairs in self.sems.items():
                for s, _ in pairs:
                    wait_for(self.view(self.me, piece), s)

    wz = Gather("w", Z, z, at_z, spatial_piece)
    wy = Gather("w", Y, y, at_y, temporal_piece)
    wait_for(own_s, own_l[0])
    wz.hop(0, 1)

    def all_to_all(src, dst, send_sem, recv_sem):
        mine = pl.ds(pl.multiple_of(seq * TB, TB), TB)

        @pl.loop(1, NSEQ)
        def _(i):
            other = lax.rem(seq + i, NSEQ)
            send(
                src.at[pl.ds(pl.multiple_of(other * TB, TB), TB)], dst.at[mine],
                send_sem, recv_sem, {"seq": other},
            )

    def rest(ref):
        return ref.at[pl.ds(0, (NSEQ - 1) * TB)]

    mine = pl.ds(pl.multiple_of(seq * TB, TB), TB)
    qkv = ((tq, tqb), (tk, tkb), (tv, tvb))
    qkv_s, qkv_r, qkv_l = [[sem("qkv") for _ in qkv] for _ in range(3)]
    for (src, dst), s, r, l in zip(qkv, qkv_s, qkv_r, qkv_l):
        all_to_all(src, dst, s, r)
        local(src.at[mine], dst.at[mine], l)

    cot_s = [sem("cot") for _ in range(X)]
    cot_r = [sem("cot") for _ in range(X - 1)]
    cot_sib = sem("cot")
    for i in range(1, X):
        send(cot, cotb.at[head], cot_s[i - 1], cot_r[i - 1], at_x(lax.rem(x + i, X)))
    send(cot, cotb.at[head], cot_s[X - 1], cot_sib, sibling)

    def heads(ref, h):
        return ref[:, h * HDIM : (h + 1) * HDIM]

    def forward(h, q, k, v, bias, shares):
        scores = dot_nt(heads(q, h), heads(k, h)) * scale + bias
        e = jnp.exp(scores - jnp.max(scores, axis=-1, keepdims=True))
        part = e * (1.0 / jnp.sum(e, axis=-1, keepdims=True))
        shares[h] = part
        return dot(part.astype(BF16), heads(v, h)).astype(BF16)

    def backward(h, q, k, v, g, shares):
        share = shares[h]
        weight = share.astype(BF16)
        grad = heads(g, h)
        grad_shares = dot_nt(grad, heads(v, h))
        centre = jnp.sum(share * grad_shares, axis=-1, keepdims=True)
        grad_scores = (share * (grad_shares - centre)).astype(BF16)
        dq = (dot(grad_scores, heads(k, h)) * scale).astype(BF16)
        dk = (dot_tn(grad_scores, heads(q, h)) * scale).astype(BF16)
        dv = dot_tn(weight, grad).astype(BF16)
        return dq, dk, dv

    for (src, dst), l in zip(spatial, spatial_l):
        wait_for(dst, l)
    NB = mask.shape[-1]
    tile = TOK // NB
    rows = lax.broadcasted_iota(jnp.int32, (TOK, TOK), 0)
    cols = lax.broadcasted_iota(jnp.int32, (TOK, TOK), 1)
    for h in range(HL):
        bias = jnp.zeros((TOK, TOK), F32)
        for a in range(NB):
            for b in range(NB):
                value = (mask[0, 0, h, a, b].astype(F32) - 1.0) * -NEG
                inside = jnp.logical_and(rows // tile == a, cols // tile == b)
                bias = jnp.where(inside, value, bias)
        s_att[:, h * HDIM : (h + 1) * HDIM] = forward(h, sq, sk, sv, bias, s_shares)

    def hop_w(j):
        for piece in range(2):
            wz.hop(piece, j)
            wy.hop(piece, j)

    wait_for(own_s, mir_r)
    wz.hop(1, 1)
    wait_for(wtt.at[y, 1], own_l[1])
    wait_for(wtt.at[y, pl.ds(0, Z // 2 - 1)], zq_r[0])
    wy.hop(0, 1)
    wait_for(wtt.at[y, pl.ds(0, Z // 2)], zq_r[1])
    wy.hop(1, 1)
    hop_w(2)

    for (src, dst), r, l in zip(qkv, qkv_r, qkv_l):
        wait_for(rest(dst), r)
        wait_for(dst.at[mine], l)
    same = jnp.where(lax.rem(rows, TB) == lax.rem(cols, TB), 0.0, NEG).astype(F32)
    for h in range(HL):
        t_att_tok[:, h * HDIM : (h + 1) * HDIM] = forward(h, tqb, tkb, tvb, same, t_shares)
    ta_s, ta_r = sem("ta"), sem("ta")
    all_to_all(t_att_tok, t_att, ta_s, ta_r)
    t_att[mine] = t_att_tok[mine]
    hop_w(3)

    fwd_s, fwd_r = [[sem("cot") for _ in range(X - 1)] for _ in range(2)]
    for i in range(1, X):
        slot = cotb.at[lax.rem(x + X - i, X) * 2 + core]
        wait_for(slot, cot_r[i - 1])
        send(slot, slot, fwd_s[i - 1], fwd_r[i - 1], sibling)
    for j in range(4, Z // 2 + 1):
        hop_w(j)
    wait_for(cotb.at[head], cot_l)
    wait_for(cotb.at[head], cot_sib)
    for i in range(1, X):
        wait_for(cotb.at[head], fwd_r[i - 1])
    wait_for(rest(t_att), ta_r)

    @pl.loop(0, Z)
    def _(b):
        both = dot_tn(cotb[b], jnp.concatenate([s_att[...], t_att[...]], axis=1)).astype(BF16)
        ps[b] = both[:, :LW].reshape(Y, Q, LW)
        pt[:, pl.ds(b, 1)] = both[:, LW:].reshape(Y, 1, Q, LW)

    class Scatter(Ring):
        def __init__(self, part, n, me, where, buf, landing):
            super().__init__(part, n, me, where)
            self.buf, self.landing = buf, landing
            size = buf.shape[1] // 2
            self.rows = [pl.ds(0, size), pl.ds(size, size)]

        def landed(self, way, piece, j):
            return self.landing.at[way, j - 1, self.rows[piece]]

        def hop(self, piece, j):
            for way in range(2):
                hops = self.hops(way, piece)
                if j <= hops:
                    dest = self.place(way, hops + 1 - j)
                    if j > 1:
                        came = self.landed(way, piece, j - 1)
                        wait_for(came, self.sems[way, piece][j - 2][1])
                        total = self.buf[dest, self.rows[piece]].astype(F32) + came[...].astype(F32)
                        self.buf[dest, self.rows[piece]] = total.astype(BF16)
                    send(
                        self.buf.at[dest, self.rows[piece]], self.landed(way, piece, j),
                        *self.sems[way, piece][j - 1], self.to[way],
                    )

        def finish(self, piece):
            total = self.buf[self.me, self.rows[piece]].astype(F32)
            for way in range(2):
                hops = self.hops(way, piece)
                came = self.landed(way, piece, hops)
                wait_for(came, self.sems[way, piece][hops - 1][1])
                total = total + came[...].astype(F32)
            self.buf[self.me, self.rows[piece]] = total.astype(BF16)

        def drain(self):
            for (way, piece), pairs in self.sems.items():
                for s, _ in pairs:
                    wait_for(self.buf.at[self.me, self.rows[piece]], s)

    rz = Scatter("p", Z, z, at_z, ps, rs_s)
    ry = Scatter("p", Y, y, at_y, pt, rs_t)

    def hop_p(j):
        for piece in range(2):
            rz.hop(piece, j)
            ry.hop(piece, j)

    hop_p(1)
    wz.finish()
    wy.finish()

    def block_t(b):
        return wtt[:, pl.ds(lax.rem(b - z + 1 + Z, Z), 1)].reshape(DH, LW)

    def block_s(b):
        return wts[b].reshape(DH, LW)

    gt_acc[...] = jnp.zeros_like(gt_acc)

    @pl.loop(0, Z)
    def _(b):
        gt_acc[...] += dot(cotb[b], block_t(b))

    g_t[...] = gt_acc[...].astype(BF16)
    gt_s, gt_r = sem("gt"), sem("gt")
    all_to_all(g_t, g_tok, gt_s, gt_r)
    g_tok[mine] = g_t[mine]
    hop_p(2)

    def update(b):
        return dot_nt(s_att[...], block_s(b)) + dot_nt(t_att[...], block_t(b))

    us_s, us_r = sem("u"), sem("u")

    @pl.loop(0, X)
    def _(i):
        u_out[i] = update(i * 2 + 1 - core).astype(BF16)
        send(u_out.at[i], u_in.at[i], us_s, us_r, sibling)

    gs_acc[...] = jnp.zeros_like(gs_acc)

    @pl.loop(0, Z)
    def _(b):
        gs_acc[...] += dot(cotb[b], block_s(b))

    hop_p(3)

    wait_for(rest(g_tok), gt_r)
    for h in range(HL):
        f = slice(h * HDIM, (h + 1) * HDIM)
        q_g[:, f], k_g[:, f], v_g[:, f] = backward(h, tqb, tkb, tvb, g_tok, t_shares)
    grads = ((q_g, gtq), (k_g, gtk), (v_g, gtv))
    grads_s, grads_r = [[sem("grads") for _ in grads] for _ in range(2)]
    for (src, dst), s, r in zip(grads, grads_s, grads_r):
        all_to_all(src, dst, s, r)
        dst[mine] = src[mine]

    @pl.loop(0, X)
    def _(i):
        u_keep[i] = update(i * 2 + core)

    wait_for(u_in, us_r)
    ux_s, ux_r = sem("u"), sem("u")

    @pl.loop(1, X)
    def _(i):
        other = lax.rem(x + i, X)
        u_send[i - 1] = (u_keep[other] + u_in[other].astype(F32)).astype(BF16)
        send(u_send.at[i - 1], u_recv.at[i - 1], ux_s, ux_r, at_x(other))

    for j in range(4, Z // 2 + 1):
        hop_p(j)

    g_s = gs_acc[...].astype(BF16)
    for h in range(HL):
        f = slice(h * HDIM, (h + 1) * HDIM)
        gsq[:, f], gsk[:, f], gsv[:, f] = backward(h, sq, sk, sv, g_s, s_shares)

    sec_ss, sec_sr, sec_ts, sec_tr = [sem("sec") for _ in range(4)]
    rz.finish(0)
    rz.finish(1)

    @pl.loop(1, Y)
    def _(i):
        other = lax.rem(y + i, Y)
        send(ps.at[z, other], sec_s.at[i - 1], sec_ss, sec_sr, at_y(other))

    ry.finish(0)
    ry.finish(1)

    @pl.loop(1, Z)
    def _(i):
        other = lax.rem(z + i, Z)
        send(pt.at[y, other], sec_t.at[i - 1], sec_ts, sec_tr, at_z(other))

    wait_for(u_recv, ux_r)
    total = u_keep[x] + u_in[x].astype(F32)
    for i in range(X - 1):
        total = total + u_recv[i].astype(F32)
    upd[...] = total.astype(BF16)

    wait_for(sec_s, sec_sr)
    total = ps[z, y].astype(F32)
    for i in range(Y - 1):
        total = total + sec_s[i].astype(F32)
    fin[dp, 0] = (total * (1.0 / NDP)).astype(BF16)
    wait_for(sec_t, sec_tr)
    total = pt[y, z].astype(F32)
    for i in range(Z - 1):
        total = total + sec_t[i].astype(F32)
    fin[dp, 1] = (total * (1.0 / NDP)).astype(BF16)

    fin_s, fin_r = sem("fin"), sem("fin")

    @pl.loop(1, NDP)
    def _(i):
        send(fin.at[dp], fin.at[dp], fin_s, fin_r, {"dp": lax.rem(dp + i, NDP)})

    for (src, dst), r in zip(grads, grads_r):
        wait_for(rest(dst), r)

    for (src, dst), s in zip(qkv, qkv_s):
        wait_for(rest(dst), s)
    wait_for(own_s, mir_s)
    wait_for(wtt.at[y, pl.ds(0, Z - 1)], zq_s)
    for s in cot_s + fwd_s:
        wait_for(cotb.at[head], s)
    wz.drain()
    wy.drain()
    rz.drain()
    ry.drain()
    for s in (ta_s, gt_s):
        wait_for(rest(t_att), s)
    for s in grads_s:
        wait_for(rest(t_att), s)
    wait_for(u_in, us_s)
    wait_for(u_recv, ux_s)
    wait_for(sec_s, sec_ss)
    wait_for(sec_t, sec_ts)
    wait_for(fin.at[pl.ds(0, NDP - 1)], fin_r)
    wait_for(fin.at[pl.ds(0, NDP - 1)], fin_s)
    gsp[...] = fin[:, 0].reshape(DS, LW).astype(F32)
    gtp[...] = fin[:, 1].reshape(DS, LW).astype(F32)


def store(*refs):
    count = len(refs) // 2
    sems = refs[-1]
    copies = [pltpu.make_async_copy(refs[i], refs[count + i], sems.at[i]) for i in range(count)]
    for copy in copies:
        copy.start()
    for copy in copies:
        copy.wait()


def per_device(dims, *args):
    NDP, NSEQ, NHEAD = dims
    sq, sk, sv, mask, tq, tk, tv, sp, tp, cot = args
    tokens, width = sq.shape[2:]
    HL = mask.shape[2]
    HDIM = width // HL
    DS, DH = sp.shape[1], cot.shape[3]
    Z, Y, X = NSEQ // 2, NDP * 2, NHEAD // 2
    Q = DS // NDP
    flat = [a.reshape(a.shape[2:]) for a in (sq, sk, sv, tq, tk, tv, cot)]
    held = flat[:6] + [p.T.reshape(NDP, Q, width) for p in (sp, tp)] + flat[6:]
    mask = pltpu.with_memory_space_constraint(mask, pltpu.HBM)
    held = [pltpu.with_memory_space_constraint(a, pltpu.HBM) for a in held]
    vmem = pl.BlockSpec(memory_space=pltpu.VMEM)
    hbm = pl.BlockSpec(memory_space=pltpu.HBM)
    feat = jax.ShapeDtypeStruct((tokens, width), BF16)
    proj = jax.ShapeDtypeStruct((DS, width), F32)

    def buf(*shape, dtype=BF16):
        return pltpu.VMEM(shape, dtype)

    feats = functools.partial(buf, tokens, width)
    out = pl.pallas_call(
        functools.partial(kernel, (NDP, NSEQ, NHEAD, HL, HDIM, Q)),
        out_shape=[jax.ShapeDtypeStruct((tokens, DH), BF16)] + [feat] * 6 + [proj] * 2,
        in_specs=[hbm] * 3 + [pl.BlockSpec(memory_space=pltpu.SMEM)] + [hbm] * 6,
        out_specs=[vmem] * 9,
        scratch_shapes=[
            feats(), feats(), feats(),
            buf(Z, Y, Q, width),
            buf(Y, Z, Q, width),
            buf(NHEAD, tokens, DH),
            feats(), feats(), feats(),
            buf(HL, tokens, tokens, dtype=F32),
            buf(HL, tokens, tokens, dtype=F32),
            feats(), feats(), feats(),
            feats(dtype=F32), feats(dtype=F32),
            feats(), feats(), feats(), feats(), feats(),
            buf(Z, Y, Q, width),
            buf(Y, Z, Q, width),
            buf(2, Z // 2, Y, Q, width),
            buf(2, Y // 2, Z, Q, width),
            buf(Y - 1, Q, width),
            buf(Z - 1, Q, width),
            buf(NDP, 2, Q, width),
            buf(X, tokens, DH),
            buf(X, tokens, DH),
            buf(X, tokens, DH, dtype=F32),
            buf(X - 1, tokens, DH),
            buf(X - 1, tokens, DH),
            pltpu.SemaphoreType.DMA((SEMS,)),
        ],
        compiler_params=pltpu.CompilerParams(
            collective_id=0, has_side_effects=True, vmem_limit_bytes=24 * 1024 * 1024
        ),
    )(*held[:3], mask, *held[3:])
    out = [pltpu.with_memory_space_constraint(o, pltpu.VMEM) for o in out]
    out = pl.pallas_call(
        store,
        out_shape=[jax.ShapeDtypeStruct(o.shape, o.dtype) for o in out],
        in_specs=[vmem] * 9,
        out_specs=[hbm] * 9,
        scratch_shapes=[pltpu.SemaphoreType.DMA((9,))],
    )(*out)
    return tuple(o[None, None] for o in out[:7]) + (out[7].T, out[8].T)


def solution(mesh):
    tokens = P("dp", "seq", None, "head")
    weights = P("head", "seq")
    dims = tuple(mesh.shape[a] for a in ("dp", "seq", "head"))
    return jax.shard_map(
        functools.partial(per_device, dims),
        mesh=mesh,
        in_specs=(tokens,) * 3 + (P("dp", "seq", "head", None, None),) + (tokens,) * 3 + (weights,) * 2 + (tokens,),
        out_specs=(tokens,) * 7 + (weights,) * 2,
        check_vma=False,
    )
```

```python
import functools
import math

import jax
import jax.numpy as jnp
from jax import lax
from jax.experimental import pallas as pl
from jax.experimental.pallas import tpu as pltpu
from jax.sharding import PartitionSpec as P

MESH = pl.DeviceIdType.MESH
BF16 = jnp.bfloat16
F32 = jnp.float32
NEG = -1e30
ORDER = (
    "sf w1 tf wz2 wy2 c wz3 wy3 cd ps pt rz1 ry1 wz4 wy4 rz2 ry2 rz3 "
    "ry3 gt wzf u1 rz4 ry4 sa ta tb u2 ss ts gs sb ud"
).split()
SEMS = 192


def dot(a, b):
    return lax.dot_general(a, b, (((1,), (0,)), ((), ())), preferred_element_type=F32)


def dot_nt(a, b):
    return lax.dot_general(a, b, (((1,), (1,)), ((), ())), preferred_element_type=F32)


def dot_tn(a, b):
    return lax.dot_general(a, b, (((0,), (0,)), ((), ())), preferred_element_type=F32)


def wait_for(view, sem):
    pltpu.make_async_copy(view, view, sem).wait()


def kernel(
    dims,
    sq_in, sk_in, sv_in, mask, tq, tk, tv, sp, tp, cot,
    upd, gsq, gsk, gsv, gtq, gtk, gtv, gsp, gtp,
    sq, sk, sv, wts, wtt, cotb, tqb, tkb, tvb,
    s_shares, t_shares, s_att, t_att, t_att_tok, gs_acc, gt_acc, g_t, g_tok, q_g, k_g, v_g,
    ps, pt, rs_s, rs_t, sec_s, sec_t, fin,
    u_out, u_in, u_keep, u_send, u_recv,
    sems,
):
    NDP, NSEQ, NHEAD, HL, HDIM, Q = dims
    Z, Y, X = NSEQ // 2, NDP * 2, NHEAD // 2
    TOK, LW = sq.shape
    DS = NDP * Q
    TB = TOK // NSEQ
    DH = cot.shape[1]
    scale = 1.0 / math.sqrt(HDIM)

    dp = lax.axis_index("dp")
    seq = lax.axis_index("seq")
    head = lax.axis_index("head")
    z, yh = seq // 2, lax.rem(seq, 2)
    y = yh * NDP + dp
    x, core = head // 2, lax.rem(head, 2)

    def at_y(place):
        return {"dp": lax.rem(place, NDP), "seq": z * 2 + place // NDP}

    def at_z(place):
        return {"seq": place * 2 + yh}

    def at_x(place):
        return {"head": place * 2 + core}

    sibling = {"head": x * 2 + 1 - core}
    counter = iter(range(SEMS))

    def sem(part):
        return sems.at[next(counter)]

    def local(src, dst, done):
        pltpu.make_async_copy(src, dst, done).start()

    def send(src, dst, send_sem, recv_sem, to):
        pltpu.make_async_remote_copy(
            src_ref=src, dst_ref=dst, send_sem=send_sem, recv_sem=recv_sem,
            device_id=to, device_id_type=MESH,
        ).start()

    barrier = pltpu.get_barrier_semaphore()

    def greet(to):
        pl.semaphore_signal(barrier, inc=1, device_id=to, device_id_type=MESH)

    @pl.loop(1, NSEQ)
    def _(i):
        greet({"seq": lax.rem(seq + i, NSEQ)})

    @pl.loop(1, NDP)
    def _(i):
        other = lax.rem(dp + i, NDP)
        greet({"dp": other, "seq": z * 2})
        greet({"dp": other, "seq": z * 2 + 1})

    @pl.loop(1, X)
    def _(i):
        greet(at_x(lax.rem(x + i, X)))

    greet(sibling)

    spatial = ((sq_in, sq), (sk_in, sk), (sv_in, sv))
    spatial_l = [sem("in") for _ in spatial]
    for (src, dst), l in zip(spatial, spatial_l):
        local(src, dst, l)
    own_l, cot_l = [sem("in") for _ in range(2)], sem("in")
    own_s = wts.at[z, pl.ds(yh * NDP, NDP)]
    local(sp, own_s, own_l[0])
    local(tp.at[dp], wtt.at[y, 1], own_l[1])
    local(cot, cotb.at[head], cot_l)

    pl.semaphore_wait(barrier, NSEQ - 1 + 2 * (NDP - 1) + X)

    def all_to_all(src, dst, send_sem, recv_sem):
        mine = pl.ds(pl.multiple_of(seq * TB, TB), TB)

        @pl.loop(1, NSEQ)
        def _(i):
            other = lax.rem(seq + i, NSEQ)
            send(
                src.at[pl.ds(pl.multiple_of(other * TB, TB), TB)], dst.at[mine],
                send_sem, recv_sem, {"seq": other},
            )

    def rest(ref):
        return ref.at[pl.ds(0, (NSEQ - 1) * TB)]

    mine = pl.ds(pl.multiple_of(seq * TB, TB), TB)
    qkv = ((tq, tqb), (tk, tkb), (tv, tvb))
    qkv_s, qkv_r, qkv_l = [[sem("qkv") for _ in qkv] for _ in range(3)]
    for (src, dst), s, r, l in zip(qkv, qkv_s, qkv_r, qkv_l):
        all_to_all(src, dst, s, r)
        local(src.at[mine], dst.at[mine], l)

    def spatial_piece(chunk, piece):
        return wts.at[chunk, pl.ds((yh if piece == 0 else 1 - yh) * NDP, NDP)]

    def temporal_piece(chunk, piece):
        return wtt.at[chunk, pl.ds(piece * (Z // 2), Z // 2)]

    zq_s, zq_r = sem("w"), [sem("w"), sem("w")]
    for i in range(1, Z):
        slot = (1 - i) % Z
        send(tp.at[dp], wtt.at[y, slot], zq_s, zq_r[slot // (Z // 2)], at_z(lax.rem(z + i, Z)))

    mir_s, mir_r = sem("w"), sem("w")
    send(sp, own_s, mir_s, mir_r, {"dp": NDP - 1 - dp, "seq": z * 2 + 1 - yh})

    class Ring:
        def __init__(self, part, n, me, where):
            self.n, self.me = n, me
            self.to = where(lax.rem(me + 1, n)), where(lax.rem(me + n - 1, n))
            self.sems = {
                (way, piece): [(sem(part), sem(part)) for _ in range(self.hops(way, piece))]
                for way in range(2) for piece in range(2)
            }

        def hops(self, way, piece):
            return self.n // 2 if way == piece else self.n // 2 - 1

        def place(self, way, k):
            return lax.rem(self.me + (k if way == 0 else -k) + self.n, self.n)

    class Gather(Ring):
        def __init__(self, part, n, me, where, view):
            super().__init__(part, n, me, where)
            self.view = view

        def arrived(self, way, piece, j):
            wait_for(self.view(self.place(way, -j), piece), self.sems[way, piece][j - 1][1])

        def hop(self, piece, j):
            for way in range(2):
                if j <= self.hops(way, piece):
                    if j > 1:
                        self.arrived(way, piece, j - 1)
                    v = self.view(self.place(way, 1 - j), piece)
                    send(v, v, *self.sems[way, piece][j - 1], self.to[way])

        def finish(self):
            for piece in range(2):
                for way in range(2):
                    self.arrived(way, piece, self.hops(way, piece))

        def drain(self):
            for (way, piece), pairs in self.sems.items():
                for s, _ in pairs:
                    wait_for(self.view(self.me, piece), s)

    wz = Gather("w", Z, z, at_z, spatial_piece)
    wy = Gather("w", Y, y, at_y, temporal_piece)
    wait_for(own_s, own_l[0])
    wz.hop(0, 1)

    cot_s = [sem("cot") for _ in range(X)]
    cot_r = [sem("cot") for _ in range(X - 1)]
    cot_sib = sem("cot")
    for i in range(1, X):
        send(cot, cotb.at[head], cot_s[i - 1], cot_r[i - 1], at_x(lax.rem(x + i, X)))
    send(cot, cotb.at[head], cot_s[X - 1], cot_sib, sibling)

    def heads(ref, h):
        return ref[:, h * HDIM : (h + 1) * HDIM]

    def forward(h, q, k, v, bias, shares):
        scores = dot_nt(heads(q, h), heads(k, h)) * scale + bias
        e = jnp.exp(scores - jnp.max(scores, axis=-1, keepdims=True))
        part = e * (1.0 / jnp.sum(e, axis=-1, keepdims=True))
        shares[h] = part
        return dot(part.astype(BF16), heads(v, h)).astype(BF16)

    def backward(h, q, k, v, g, shares):
        share = shares[h]
        weight = share.astype(BF16)
        grad = heads(g, h)
        grad_shares = dot_nt(grad, heads(v, h))
        centre = jnp.sum(share * grad_shares, axis=-1, keepdims=True)
        grad_scores = (share * (grad_shares - centre)).astype(BF16)
        dq = (dot(grad_scores, heads(k, h)) * scale).astype(BF16)
        dk = (dot_tn(grad_scores, heads(q, h)) * scale).astype(BF16)
        dv = dot_tn(weight, grad).astype(BF16)
        return dq, dk, dv

    class Scatter(Ring):
        def __init__(self, part, n, me, where, buf, landing):
            super().__init__(part, n, me, where)
            self.buf, self.landing = buf, landing
            size = buf.shape[1] // 2
            self.rows = [pl.ds(0, size), pl.ds(size, size)]

        def landed(self, way, piece, j):
            return self.landing.at[way, j - 1, self.rows[piece]]

        def hop(self, piece, j):
            for way in range(2):
                hops = self.hops(way, piece)
                if j <= hops:
                    dest = self.place(way, hops + 1 - j)
                    if j > 1:
                        came = self.landed(way, piece, j - 1)
                        wait_for(came, self.sems[way, piece][j - 2][1])
                        total = self.buf[dest, self.rows[piece]].astype(F32) + came[...].astype(F32)
                        self.buf[dest, self.rows[piece]] = total.astype(BF16)
                    send(
                        self.buf.at[dest, self.rows[piece]], self.landed(way, piece, j),
                        *self.sems[way, piece][j - 1], self.to[way],
                    )

        def finish(self, piece):
            total = self.buf[self.me, self.rows[piece]].astype(F32)
            for way in range(2):
                hops = self.hops(way, piece)
                came = self.landed(way, piece, hops)
                wait_for(came, self.sems[way, piece][hops - 1][1])
                total = total + came[...].astype(F32)
            self.buf[self.me, self.rows[piece]] = total.astype(BF16)

        def drain(self):
            for (way, piece), pairs in self.sems.items():
                for s, _ in pairs:
                    wait_for(self.buf.at[self.me, self.rows[piece]], s)

    rz = Scatter("p", Z, z, at_z, ps, rs_s)
    ry = Scatter("p", Y, y, at_y, pt, rs_t)

    def block_t(b):
        return wtt[:, pl.ds(lax.rem(b - z + 1 + Z, Z), 1)].reshape(DH, LW)

    def block_s(b):
        return wts[b].reshape(DH, LW)

    def update(b):
        return dot_nt(s_att[...], block_s(b)) + dot_nt(t_att[...], block_t(b))

    rows = lax.broadcasted_iota(jnp.int32, (TOK, TOK), 0)
    cols = lax.broadcasted_iota(jnp.int32, (TOK, TOK), 1)
    ta_s, ta_r, gt_s, gt_r = sem("ta"), sem("ta"), sem("gt"), sem("gt")
    fwd_s, fwd_r = [[sem("cot") for _ in range(X - 1)] for _ in range(2)]
    us_s, us_r, ux_s, ux_r = [sem("u") for _ in range(4)]
    grads = ((q_g, gtq), (k_g, gtk), (v_g, gtv))
    grads_s, grads_r = [[sem("grads") for _ in grads] for _ in range(2)]
    sec_ss, sec_sr, sec_ts, sec_tr = [sem("sec") for _ in range(4)]
    fin_ss, fin_sr, fin_ts, fin_tr = [sem("fin") for _ in range(4)]

    def spatial_forward():
        for (src, dst), l in zip(spatial, spatial_l):
            wait_for(dst, l)
        NB = mask.shape[-1]
        tile = TOK // NB
        for h in range(HL):
            bias = jnp.zeros((TOK, TOK), F32)
            for a in range(NB):
                for b in range(NB):
                    value = (mask[0, 0, h, a, b].astype(F32) - 1.0) * -NEG
                    inside = jnp.logical_and(rows // tile == a, cols // tile == b)
                    bias = jnp.where(inside, value, bias)
            s_att[:, h * HDIM : (h + 1) * HDIM] = forward(h, sq, sk, sv, bias, s_shares)

    def weights_start():
        wait_for(own_s, mir_r)
        wz.hop(1, 1)
        wait_for(wtt.at[y, 1], own_l[1])
        wait_for(wtt.at[y, pl.ds(0, Z // 2 - 1)], zq_r[0])
        wy.hop(0, 1)
        wait_for(wtt.at[y, pl.ds(0, Z // 2)], zq_r[1])
        wy.hop(1, 1)

    def temporal_forward():
        for (src, dst), r, l in zip(qkv, qkv_r, qkv_l):
            wait_for(rest(dst), r)
            wait_for(dst.at[mine], l)
        same = jnp.where(lax.rem(rows, TB) == lax.rem(cols, TB), 0.0, NEG).astype(F32)
        for h in range(HL):
            t_att_tok[:, h * HDIM : (h + 1) * HDIM] = forward(h, tqb, tkb, tvb, same, t_shares)
        all_to_all(t_att_tok, t_att, ta_s, ta_r)
        t_att[mine] = t_att_tok[mine]

    def cotangent_on():
        for i in range(1, X):
            slot = cotb.at[lax.rem(x + X - i, X) * 2 + core]
            wait_for(slot, cot_r[i - 1])
            send(slot, slot, fwd_s[i - 1], fwd_r[i - 1], sibling)

    def cotangent_done():
        wait_for(cotb.at[head], cot_l)
        wait_for(cotb.at[head], cot_sib)
        for i in range(1, X):
            wait_for(cotb.at[head], fwd_r[i - 1])

    def spatial_product():
        @pl.loop(0, Z)
        def _(b):
            ps[b] = dot_tn(cotb[b], s_att[...]).astype(BF16).reshape(Y, Q, LW)

    def temporal_product():
        wait_for(rest(t_att), ta_r)

        @pl.loop(0, Z)
        def _(b):
            pt[:, pl.ds(b, 1)] = dot_tn(cotb[b], t_att[...]).astype(BF16).reshape(Y, 1, Q, LW)

    def temporal_gradient():
        wy.finish()
        gt_acc[...] = jnp.zeros_like(gt_acc)

        @pl.loop(0, Z)
        def _(b):
            gt_acc[...] += dot(cotb[b], block_t(b))

        g_t[...] = gt_acc[...].astype(BF16)
        all_to_all(g_t, g_tok, gt_s, gt_r)
        g_tok[mine] = g_t[mine]

    def spatial_gradient():
        gs_acc[...] = jnp.zeros_like(gs_acc)

        @pl.loop(0, Z)
        def _(b):
            gs_acc[...] += dot(cotb[b], block_s(b))

    def update_other():
        @pl.loop(0, X)
        def _(i):
            u_out[i] = update(i * 2 + 1 - core).astype(BF16)
            send(u_out.at[i], u_in.at[i], us_s, us_r, sibling)

    def update_own():
        @pl.loop(0, X)
        def _(i):
            u_keep[i] = update(i * 2 + core)

        wait_for(u_in, us_r)

        @pl.loop(1, X)
        def _(i):
            other = lax.rem(x + i, X)
            u_send[i - 1] = (u_keep[other] + u_in[other].astype(F32)).astype(BF16)
            send(u_send.at[i - 1], u_recv.at[i - 1], ux_s, ux_r, at_x(other))

    def update_done():
        wait_for(u_recv, ux_r)
        total = u_keep[x] + u_in[x].astype(F32)
        for i in range(X - 1):
            total = total + u_recv[i].astype(F32)
        upd[...] = total.astype(BF16)

    def temporal_backward():
        wait_for(rest(g_tok), gt_r)
        for h in range(HL):
            f = slice(h * HDIM, (h + 1) * HDIM)
            q_g[:, f], k_g[:, f], v_g[:, f] = backward(h, tqb, tkb, tvb, g_tok, t_shares)
        for (src, dst), s, r in zip(grads, grads_s, grads_r):
            all_to_all(src, dst, s, r)
            dst[mine] = src[mine]

    def spatial_backward():
        g_s = gs_acc[...].astype(BF16)
        for h in range(HL):
            f = slice(h * HDIM, (h + 1) * HDIM)
            gsq[:, f], gsk[:, f], gsv[:, f] = backward(h, sq, sk, sv, g_s, s_shares)

    def spatial_across():
        rz.finish(0)
        rz.finish(1)

        @pl.loop(1, Y)
        def _(i):
            other = lax.rem(y + i, Y)
            send(ps.at[z, other], sec_s.at[i - 1], sec_ss, sec_sr, at_y(other))

    def temporal_across():
        ry.finish(0)
        ry.finish(1)

        @pl.loop(1, Z)
        def _(i):
            other = lax.rem(z + i, Z)
            send(pt.at[y, other], sec_t.at[i - 1], sec_ts, sec_tr, at_z(other))

    def share(own, parts, count, slot, left, came):
        total = own.astype(F32)
        for i in range(count - 1):
            total = total + parts[i].astype(F32)
        fin[slot, dp] = (total * (1.0 / NDP)).astype(BF16)

        @pl.loop(1, NDP)
        def _(i):
            send(fin.at[slot, dp], fin.at[slot, dp], left, came, {"dp": lax.rem(dp + i, NDP)})

    def spatial_share():
        wait_for(sec_s, sec_sr)
        share(ps[z, y], sec_s, Y, 0, fin_ss, fin_sr)

    def temporal_share():
        wait_for(sec_t, sec_tr)
        share(pt[y, z], sec_t, Z, 1, fin_ts, fin_tr)

    steps = {
        "sf": spatial_forward, "w1": weights_start, "tf": temporal_forward, "c": cotangent_on, "cd": cotangent_done,
        "ps": spatial_product, "pt": temporal_product, "gt": temporal_gradient, "gs": spatial_gradient,
        "wzf": wz.finish, "u1": update_other, "u2": update_own, "ud": update_done, "tb": temporal_backward,
        "sb": spatial_backward, "sa": spatial_across, "ta": temporal_across, "ss": spatial_share, "ts": temporal_share,
    }
    rings = {"wz": wz, "wy": wy, "rz": rz, "ry": ry}
    for name in ORDER:
        if name in steps:
            steps[name]()
        else:
            for piece in range(2):
                rings[name[:2]].hop(piece, int(name[2:]))
    for (src, dst), r in zip(grads, grads_r):
        wait_for(rest(dst), r)

    for (src, dst), s in zip(qkv, qkv_s):
        wait_for(rest(dst), s)
    wait_for(own_s, mir_s)
    wait_for(wtt.at[y, pl.ds(0, Z - 1)], zq_s)
    for s in cot_s + fwd_s:
        wait_for(cotb.at[head], s)
    wz.drain()
    wy.drain()
    rz.drain()
    ry.drain()
    for s in (ta_s, gt_s):
        wait_for(rest(t_att), s)
    for s in grads_s:
        wait_for(rest(t_att), s)
    wait_for(u_in, us_s)
    wait_for(u_recv, ux_s)
    wait_for(sec_s, sec_ss)
    wait_for(sec_t, sec_ts)
    for slot, left, came, out in ((0, fin_ss, fin_sr, gsp), (1, fin_ts, fin_tr, gtp)):
        wait_for(fin.at[slot, pl.ds(0, NDP - 1)], came)
        wait_for(fin.at[slot, pl.ds(0, NDP - 1)], left)
        out[...] = fin[slot].reshape(DS, LW).astype(F32)


def store(*refs):
    count = len(refs) // 2
    sems = refs[-1]
    copies = [pltpu.make_async_copy(refs[i], refs[count + i], sems.at[i]) for i in range(count)]
    for copy in copies:
        copy.start()
    for copy in copies:
        copy.wait()


def per_device(dims, *args):
    NDP, NSEQ, NHEAD = dims
    sq, sk, sv, mask, tq, tk, tv, sp, tp, cot = args
    tokens, width = sq.shape[2:]
    HL = mask.shape[2]
    HDIM = width // HL
    DS, DH = sp.shape[1], cot.shape[3]
    Z, Y, X = NSEQ // 2, NDP * 2, NHEAD // 2
    Q = DS // NDP
    flat = [a.reshape(a.shape[2:]) for a in (sq, sk, sv, tq, tk, tv, cot)]
    held = flat[:6] + [p.T.reshape(NDP, Q, width) for p in (sp, tp)] + flat[6:]
    mask = pltpu.with_memory_space_constraint(mask, pltpu.HBM)
    held = [pltpu.with_memory_space_constraint(a, pltpu.HBM) for a in held]
    vmem = pl.BlockSpec(memory_space=pltpu.VMEM)
    hbm = pl.BlockSpec(memory_space=pltpu.HBM)
    feat = jax.ShapeDtypeStruct((tokens, width), BF16)
    proj = jax.ShapeDtypeStruct((DS, width), F32)

    def buf(*shape, dtype=BF16):
        return pltpu.VMEM(shape, dtype)

    feats = functools.partial(buf, tokens, width)
    out = pl.pallas_call(
        functools.partial(kernel, (NDP, NSEQ, NHEAD, HL, HDIM, Q)),
        out_shape=[jax.ShapeDtypeStruct((tokens, DH), BF16)] + [feat] * 6 + [proj] * 2,
        in_specs=[hbm] * 3 + [pl.BlockSpec(memory_space=pltpu.SMEM)] + [hbm] * 6,
        out_specs=[vmem] * 9,
        scratch_shapes=[
            feats(), feats(), feats(),
            buf(Z, Y, Q, width),
            buf(Y, Z, Q, width),
            buf(NHEAD, tokens, DH),
            feats(), feats(), feats(),
            buf(HL, tokens, tokens, dtype=F32),
            buf(HL, tokens, tokens, dtype=F32),
            feats(), feats(), feats(),
            feats(dtype=F32), feats(dtype=F32),
            feats(), feats(), feats(), feats(), feats(),
            buf(Z, Y, Q, width),
            buf(Y, Z, Q, width),
            buf(2, Z // 2, Y, Q, width),
            buf(2, Y // 2, Z, Q, width),
            buf(Y - 1, Q, width),
            buf(Z - 1, Q, width),
            buf(2, NDP, Q, width),
            buf(X, tokens, DH),
            buf(X, tokens, DH),
            buf(X, tokens, DH, dtype=F32),
            buf(X - 1, tokens, DH),
            buf(X - 1, tokens, DH),
            pltpu.SemaphoreType.DMA((SEMS,)),
        ],
        compiler_params=pltpu.CompilerParams(
            collective_id=0, has_side_effects=True, vmem_limit_bytes=24 * 1024 * 1024
        ),
    )(*held[:3], mask, *held[3:])
    out = [pltpu.with_memory_space_constraint(o, pltpu.VMEM) for o in out]
    out = pl.pallas_call(
        store,
        out_shape=[jax.ShapeDtypeStruct(o.shape, o.dtype) for o in out],
        in_specs=[vmem] * 9,
        out_specs=[hbm] * 9,
        scratch_shapes=[pltpu.SemaphoreType.DMA((9,))],
    )(*out)
    return tuple(o[None, None] for o in out[:7]) + (out[7].T, out[8].T)


def solution(mesh):
    tokens = P("dp", "seq", None, "head")
    weights = P("head", "seq")
    dims = tuple(mesh.shape[a] for a in ("dp", "seq", "head"))
    return jax.shard_map(
        functools.partial(per_device, dims),
        mesh=mesh,
        in_specs=(tokens,) * 3 + (P("dp", "seq", "head", None, None),) + (tokens,) * 3 + (weights,) * 2 + (tokens,),
        out_specs=(tokens,) * 7 + (weights,) * 2,
        check_vma=False,
    )
```

```python
import functools
import math

import jax
import jax.numpy as jnp
from jax import lax
from jax.experimental import pallas as pl
from jax.experimental.pallas import tpu as pltpu
from jax.sharding import PartitionSpec as P

MESH = pl.DeviceIdType.MESH
BF16 = jnp.bfloat16
F32 = jnp.float32
NEG = -1e30
ORDER = (
    "sf", "w1", "tf", "wz2", "wy2", "c", "wz3", "wy3", "cd", "ps", "pt", "rz1", "ry1", "wz4", "wy4", "rz2", "ry2",
    "rz3", "ry3", "gt", "wzf", "u1", "rz4", "ry4", "sa", "ta", "tb", "u2", "ss", "ts", "gs", "sb", "ud",
)
SEMS = 192


def dot(a, b):
    return lax.dot_general(a, b, (((1,), (0,)), ((), ())), preferred_element_type=F32)


def dot_nt(a, b):
    return lax.dot_general(a, b, (((1,), (1,)), ((), ())), preferred_element_type=F32)


def dot_tn(a, b):
    return lax.dot_general(a, b, (((0,), (0,)), ((), ())), preferred_element_type=F32)


def wait_for(view, sem):
    pltpu.make_async_copy(view, view, sem).wait()


def kernel(
    dims,
    sq_in, sk_in, sv_in, mask, tq, tk, tv, sp, tp, cot,
    upd, gsq, gsk, gsv, gtq, gtk, gtv, gsp, gtp,
    sq, sk, sv, wts, wtt, cotb, tqb, tkb, tvb,
    s_shares, t_shares, s_att, t_att, t_att_tok, gs_acc, gt_acc, g_t, g_tok, q_g, k_g, v_g,
    ps, pt, rs_s, rs_t, sec_s, sec_t, fin,
    u_out, u_in, u_keep, u_send, u_recv,
    sems,
):
    NDP, NSEQ, NHEAD, HL, HDIM, Q = dims
    Z, Y, X = NSEQ // 2, NDP * 2, NHEAD // 2
    TOK, LW = sq.shape
    DS = NDP * Q
    TB = TOK // NSEQ
    DH = cot.shape[1]
    scale = 1.0 / math.sqrt(HDIM)

    dp = lax.axis_index("dp")
    seq = lax.axis_index("seq")
    head = lax.axis_index("head")
    z, yh = seq // 2, lax.rem(seq, 2)
    y = yh * NDP + dp
    x, core = head // 2, lax.rem(head, 2)

    def at_y(place):
        return {"dp": lax.rem(place, NDP), "seq": z * 2 + place // NDP}

    def at_z(place):
        return {"seq": place * 2 + yh}

    def at_x(place):
        return {"head": place * 2 + core}

    sibling = {"head": x * 2 + 1 - core}
    counter = iter(range(SEMS))

    def sem(part):
        return sems.at[next(counter)]

    def local(src, dst, done):
        pltpu.make_async_copy(src, dst, done).start()

    def send(src, dst, send_sem, recv_sem, to):
        pltpu.make_async_remote_copy(
            src_ref=src, dst_ref=dst, send_sem=send_sem, recv_sem=recv_sem,
            device_id=to, device_id_type=MESH,
        ).start()

    barrier = pltpu.get_barrier_semaphore()

    def greet(to):
        pl.semaphore_signal(barrier, inc=1, device_id=to, device_id_type=MESH)

    @pl.loop(1, NSEQ)
    def _(i):
        greet({"seq": lax.rem(seq + i, NSEQ)})

    @pl.loop(1, NDP)
    def _(i):
        other = lax.rem(dp + i, NDP)
        greet({"dp": other, "seq": z * 2})
        greet({"dp": other, "seq": z * 2 + 1})

    @pl.loop(1, X)
    def _(i):
        greet(at_x(lax.rem(x + i, X)))

    greet(sibling)

    spatial = ((sq_in, sq), (sk_in, sk), (sv_in, sv))
    spatial_l = [sem("in") for _ in spatial]
    for (src, dst), l in zip(spatial, spatial_l):
        local(src, dst, l)
    own_l, cot_l = [sem("in") for _ in range(2)], sem("in")
    own_s = wts.at[z, pl.ds(yh * NDP, NDP)]
    local(sp, own_s, own_l[0])
    local(tp.at[dp], wtt.at[y, 1], own_l[1])
    local(cot, cotb.at[head], cot_l)

    pl.semaphore_wait(barrier, NSEQ - 1 + 2 * (NDP - 1) + X)

    def all_to_all(src, dst, send_sem, recv_sem):
        mine = pl.ds(pl.multiple_of(seq * TB, TB), TB)

        @pl.loop(1, NSEQ)
        def _(i):
            other = lax.rem(seq + i, NSEQ)
            send(
                src.at[pl.ds(pl.multiple_of(other * TB, TB), TB)], dst.at[mine],
                send_sem, recv_sem, {"seq": other},
            )

    def rest(ref):
        return ref.at[pl.ds(0, (NSEQ - 1) * TB)]

    mine = pl.ds(pl.multiple_of(seq * TB, TB), TB)
    qkv = ((tq, tqb), (tk, tkb), (tv, tvb))
    qkv_s, qkv_r, qkv_l = [[sem("qkv") for _ in qkv] for _ in range(3)]
    for (src, dst), s, r, l in zip(qkv, qkv_s, qkv_r, qkv_l):
        all_to_all(src, dst, s, r)
        local(src.at[mine], dst.at[mine], l)

    def spatial_piece(chunk, piece):
        return wts.at[chunk, pl.ds((yh if piece == 0 else 1 - yh) * NDP, NDP)]

    def temporal_piece(chunk, piece):
        return wtt.at[chunk, pl.ds(piece * (Z // 2), Z // 2)]

    zq_s, zq_r = sem("w"), [sem("w"), sem("w")]
    for i in range(1, Z):
        slot = (1 - i) % Z
        send(tp.at[dp], wtt.at[y, slot], zq_s, zq_r[slot // (Z // 2)], at_z(lax.rem(z + i, Z)))

    mir_s, mir_r = sem("w"), sem("w")
    send(sp, own_s, mir_s, mir_r, {"dp": NDP - 1 - dp, "seq": z * 2 + 1 - yh})

    class Ring:
        def __init__(self, part, n, me, where):
            self.n, self.me = n, me
            self.to = where(lax.rem(me + 1, n)), where(lax.rem(me + n - 1, n))
            self.sems = {
                (way, piece): [(sem(part), sem(part)) for _ in range(self.hops(way, piece))]
                for way in range(2) for piece in range(2)
            }

        def hops(self, way, piece):
            return self.n // 2 if way == piece else self.n // 2 - 1

        def place(self, way, k):
            return lax.rem(self.me + (k if way == 0 else -k) + self.n, self.n)

    class Gather(Ring):
        def __init__(self, part, n, me, where, view):
            super().__init__(part, n, me, where)
            self.view = view

        def arrived(self, way, piece, j):
            wait_for(self.view(self.place(way, -j), piece), self.sems[way, piece][j - 1][1])

        def hop(self, piece, j):
            for way in range(2):
                if j <= self.hops(way, piece):
                    if j > 1:
                        self.arrived(way, piece, j - 1)
                    v = self.view(self.place(way, 1 - j), piece)
                    send(v, v, *self.sems[way, piece][j - 1], self.to[way])

        def finish(self):
            for piece in range(2):
                for way in range(2):
                    self.arrived(way, piece, self.hops(way, piece))

        def drain(self):
            for (way, piece), pairs in self.sems.items():
                for s, _ in pairs:
                    wait_for(self.view(self.me, piece), s)

    wz = Gather("w", Z, z, at_z, spatial_piece)
    wy = Gather("w", Y, y, at_y, temporal_piece)
    wait_for(own_s, own_l[0])
    wz.hop(0, 1)

    cot_s = [sem("cot") for _ in range(X)]
    cot_r = [sem("cot") for _ in range(X - 1)]
    cot_sib = sem("cot")
    for i in range(1, X):
        send(cot, cotb.at[head], cot_s[i - 1], cot_r[i - 1], at_x(lax.rem(x + i, X)))
    send(cot, cotb.at[head], cot_s[X - 1], cot_sib, sibling)

    def heads(ref, h):
        return ref[:, h * HDIM : (h + 1) * HDIM]

    def forward(h, q, k, v, bias, shares):
        scores = dot_nt(heads(q, h), heads(k, h)) * scale + bias
        e = jnp.exp(scores - jnp.max(scores, axis=-1, keepdims=True))
        part = e * (1.0 / jnp.sum(e, axis=-1, keepdims=True))
        shares[h] = part
        return dot(part.astype(BF16), heads(v, h)).astype(BF16)

    def backward(h, q, k, v, g, shares):
        share = shares[h]
        weight = share.astype(BF16)
        grad = heads(g, h)
        grad_shares = dot_nt(grad, heads(v, h))
        centre = jnp.sum(share * grad_shares, axis=-1, keepdims=True)
        grad_scores = (share * (grad_shares - centre)).astype(BF16)
        dq = (dot(grad_scores, heads(k, h)) * scale).astype(BF16)
        dk = (dot_tn(grad_scores, heads(q, h)) * scale).astype(BF16)
        dv = dot_tn(weight, grad).astype(BF16)
        return dq, dk, dv

    class Scatter(Ring):
        def __init__(self, part, n, me, where, buf, landing):
            super().__init__(part, n, me, where)
            self.buf, self.landing = buf, landing
            size = buf.shape[1] // 2
            self.rows = [pl.ds(0, size), pl.ds(size, size)]

        def landed(self, way, piece, j):
            return self.landing.at[way, j - 1, self.rows[piece]]

        def hop(self, piece, j):
            for way in range(2):
                hops = self.hops(way, piece)
                if j <= hops:
                    dest = self.place(way, hops + 1 - j)
                    if j > 1:
                        came = self.landed(way, piece, j - 1)
                        wait_for(came, self.sems[way, piece][j - 2][1])
                        total = self.buf[dest, self.rows[piece]].astype(F32) + came[...].astype(F32)
                        self.buf[dest, self.rows[piece]] = total.astype(BF16)
                    send(
                        self.buf.at[dest, self.rows[piece]], self.landed(way, piece, j),
                        *self.sems[way, piece][j - 1], self.to[way],
                    )

        def finish(self, piece):
            total = self.buf[self.me, self.rows[piece]].astype(F32)
            for way in range(2):
                hops = self.hops(way, piece)
                came = self.landed(way, piece, hops)
                wait_for(came, self.sems[way, piece][hops - 1][1])
                total = total + came[...].astype(F32)
            self.buf[self.me, self.rows[piece]] = total.astype(BF16)

        def drain(self):
            for (way, piece), pairs in self.sems.items():
                for s, _ in pairs:
                    wait_for(self.buf.at[self.me, self.rows[piece]], s)

    rz = Scatter("p", Z, z, at_z, ps, rs_s)
    ry = Scatter("p", Y, y, at_y, pt, rs_t)

    def block_t(b):
        return wtt[:, pl.ds(lax.rem(b - z + 1 + Z, Z), 1)].reshape(DH, LW)

    def block_s(b):
        return wts[b].reshape(DH, LW)

    def update(b):
        return dot_nt(s_att[...], block_s(b)) + dot_nt(t_att[...], block_t(b))

    rows = lax.broadcasted_iota(jnp.int32, (TOK, TOK), 0)
    cols = lax.broadcasted_iota(jnp.int32, (TOK, TOK), 1)
    ta_s, ta_r, gt_s, gt_r = sem("ta"), sem("ta"), sem("gt"), sem("gt")
    fwd_s, fwd_r = [[sem("cot") for _ in range(X - 1)] for _ in range(2)]
    us_s, us_r, ux_s, ux_r = [sem("u") for _ in range(4)]
    grads = ((q_g, gtq), (k_g, gtk), (v_g, gtv))
    grads_s, grads_r = [[sem("grads") for _ in grads] for _ in range(2)]
    sec_ss, sec_sr, sec_ts, sec_tr = [sem("sec") for _ in range(4)]
    fin_ss, fin_sr, fin_ts, fin_tr = [sem("fin") for _ in range(4)]

    def spatial_forward():
        for (src, dst), l in zip(spatial, spatial_l):
            wait_for(dst, l)
        NB = mask.shape[-1]
        tile = TOK // NB
        for h in range(HL):
            bias = jnp.zeros((TOK, TOK), F32)
            for a in range(NB):
                for b in range(NB):
                    value = (mask[0, 0, h, a, b].astype(F32) - 1.0) * -NEG
                    inside = jnp.logical_and(rows // tile == a, cols // tile == b)
                    bias = jnp.where(inside, value, bias)
            s_att[:, h * HDIM : (h + 1) * HDIM] = forward(h, sq, sk, sv, bias, s_shares)

    def weights_start():
        wait_for(own_s, mir_r)
        wz.hop(1, 1)
        wait_for(wtt.at[y, 1], own_l[1])
        wait_for(wtt.at[y, pl.ds(0, Z // 2 - 1)], zq_r[0])
        wy.hop(0, 1)
        wait_for(wtt.at[y, pl.ds(0, Z // 2)], zq_r[1])
        wy.hop(1, 1)

    def temporal_forward():
        for (src, dst), r, l in zip(qkv, qkv_r, qkv_l):
            wait_for(rest(dst), r)
            wait_for(dst.at[mine], l)
        same = jnp.where(lax.rem(rows, TB) == lax.rem(cols, TB), 0.0, NEG).astype(F32)
        for h in range(HL):
            t_att_tok[:, h * HDIM : (h + 1) * HDIM] = forward(h, tqb, tkb, tvb, same, t_shares)
        all_to_all(t_att_tok, t_att, ta_s, ta_r)
        t_att[mine] = t_att_tok[mine]

    def cotangent_on():
        for i in range(1, X):
            slot = cotb.at[lax.rem(x + X - i, X) * 2 + core]
            wait_for(slot, cot_r[i - 1])
            send(slot, slot, fwd_s[i - 1], fwd_r[i - 1], sibling)

    def cotangent_done():
        wait_for(cotb.at[head], cot_l)
        wait_for(cotb.at[head], cot_sib)
        for i in range(1, X):
            wait_for(cotb.at[head], fwd_r[i - 1])

    def spatial_product():
        @pl.loop(0, Z)
        def _(b):
            ps[b] = dot_tn(cotb[b], s_att[...]).astype(BF16).reshape(Y, Q, LW)

    def temporal_product():
        wait_for(rest(t_att), ta_r)

        @pl.loop(0, Z)
        def _(b):
            pt[:, pl.ds(b, 1)] = dot_tn(cotb[b], t_att[...]).astype(BF16).reshape(Y, 1, Q, LW)

    def temporal_gradient():
        wy.finish()
        gt_acc[...] = jnp.zeros_like(gt_acc)

        @pl.loop(0, Z)
        def _(b):
            gt_acc[...] += dot(cotb[b], block_t(b))

        g_t[...] = gt_acc[...].astype(BF16)
        all_to_all(g_t, g_tok, gt_s, gt_r)
        g_tok[mine] = g_t[mine]

    def spatial_gradient():
        gs_acc[...] = jnp.zeros_like(gs_acc)

        @pl.loop(0, Z)
        def _(b):
            gs_acc[...] += dot(cotb[b], block_s(b))

    def update_other():
        @pl.loop(0, X)
        def _(i):
            u_out[i] = update(i * 2 + 1 - core).astype(BF16)
            send(u_out.at[i], u_in.at[i], us_s, us_r, sibling)

    def update_own():
        @pl.loop(0, X)
        def _(i):
            u_keep[i] = update(i * 2 + core)

        wait_for(u_in, us_r)

        @pl.loop(1, X)
        def _(i):
            other = lax.rem(x + i, X)
            u_send[i - 1] = (u_keep[other] + u_in[other].astype(F32)).astype(BF16)
            send(u_send.at[i - 1], u_recv.at[i - 1], ux_s, ux_r, at_x(other))

    def update_done():
        wait_for(u_recv, ux_r)
        total = u_keep[x] + u_in[x].astype(F32)
        for i in range(X - 1):
            total = total + u_recv[i].astype(F32)
        upd[...] = total.astype(BF16)

    def temporal_backward():
        wait_for(rest(g_tok), gt_r)
        for h in range(HL):
            f = slice(h * HDIM, (h + 1) * HDIM)
            q_g[:, f], k_g[:, f], v_g[:, f] = backward(h, tqb, tkb, tvb, g_tok, t_shares)
        for (src, dst), s, r in zip(grads, grads_s, grads_r):
            all_to_all(src, dst, s, r)
            dst[mine] = src[mine]

    def spatial_backward():
        g_s = gs_acc[...].astype(BF16)
        for h in range(HL):
            f = slice(h * HDIM, (h + 1) * HDIM)
            gsq[:, f], gsk[:, f], gsv[:, f] = backward(h, sq, sk, sv, g_s, s_shares)

    def across(ring, buf, mine, me, n, landing, left, came, where):
        for piece in range(2):
            ring.finish(piece)

            @pl.loop(piece * (n // 2), (piece + 1) * (n // 2))
            def _(other):
                @pl.when(other != me)
                def _():
                    slot = lax.rem(other - me + n, n) - 1
                    send(buf.at[mine, other], landing.at[slot], left, came, where(other))

    def spatial_across():
        across(rz, ps, z, y, Y, sec_s, sec_ss, sec_sr, at_y)

    def temporal_across():
        across(ry, pt, y, z, Z, sec_t, sec_ts, sec_tr, at_z)

    def share(own, parts, count, slot, left, came):
        total = own.astype(F32)
        for i in range(count - 1):
            total = total + parts[i].astype(F32)
        fin[slot, dp] = (total * (1.0 / NDP)).astype(BF16)

        @pl.loop(1, NDP)
        def _(i):
            send(fin.at[slot, dp], fin.at[slot, dp], left, came, {"dp": lax.rem(dp + i, NDP)})

    def spatial_share():
        wait_for(sec_s, sec_sr)
        share(ps[z, y], sec_s, Y, 0, fin_ss, fin_sr)

    def temporal_share():
        wait_for(sec_t, sec_tr)
        share(pt[y, z], sec_t, Z, 1, fin_ts, fin_tr)

    steps = {
        "sf": spatial_forward, "w1": weights_start, "tf": temporal_forward, "c": cotangent_on, "cd": cotangent_done,
        "ps": spatial_product, "pt": temporal_product, "gt": temporal_gradient, "gs": spatial_gradient,
        "wzf": wz.finish, "u1": update_other, "u2": update_own, "ud": update_done, "tb": temporal_backward,
        "sb": spatial_backward, "sa": spatial_across, "ta": temporal_across, "ss": spatial_share, "ts": temporal_share,
    }
    rings = {"wz": wz, "wy": wy, "rz": rz, "ry": ry}
    for name in ORDER:
        if name in steps:
            steps[name]()
        else:
            for piece in range(2):
                rings[name[:2]].hop(piece, int(name[2:]))
    for (src, dst), r in zip(grads, grads_r):
        wait_for(rest(dst), r)

    for (src, dst), s in zip(qkv, qkv_s):
        wait_for(rest(dst), s)
    wait_for(own_s, mir_s)
    wait_for(wtt.at[y, pl.ds(0, Z - 1)], zq_s)
    for s in cot_s + fwd_s:
        wait_for(cotb.at[head], s)
    wz.drain()
    wy.drain()
    rz.drain()
    ry.drain()
    for s in (ta_s, gt_s):
        wait_for(rest(t_att), s)
    for s in grads_s:
        wait_for(rest(t_att), s)
    wait_for(u_in, us_s)
    wait_for(u_recv, ux_s)
    wait_for(sec_s, sec_ss)
    wait_for(sec_t, sec_ts)
    for slot, left, came, out in ((0, fin_ss, fin_sr, gsp), (1, fin_ts, fin_tr, gtp)):
        wait_for(fin.at[slot, pl.ds(0, NDP - 1)], came)
        wait_for(fin.at[slot, pl.ds(0, NDP - 1)], left)
        out[...] = fin[slot].reshape(DS, LW).astype(F32)


def store(*refs):
    count = len(refs) // 2
    sems = refs[-1]
    copies = [pltpu.make_async_copy(refs[i], refs[count + i], sems.at[i]) for i in range(count)]
    for copy in copies:
        copy.start()
    for copy in copies:
        copy.wait()


def per_device(dims, *args):
    NDP, NSEQ, NHEAD = dims
    sq, sk, sv, mask, tq, tk, tv, sp, tp, cot = args
    tokens, width = sq.shape[2:]
    HL = mask.shape[2]
    HDIM = width // HL
    DS, DH = sp.shape[1], cot.shape[3]
    Z, Y, X = NSEQ // 2, NDP * 2, NHEAD // 2
    Q = DS // NDP
    flat = [a.reshape(a.shape[2:]) for a in (sq, sk, sv, tq, tk, tv, cot)]
    held = flat[:6] + [p.T.reshape(NDP, Q, width) for p in (sp, tp)] + flat[6:]
    mask = pltpu.with_memory_space_constraint(mask, pltpu.HBM)
    held = [pltpu.with_memory_space_constraint(a, pltpu.HBM) for a in held]
    vmem = pl.BlockSpec(memory_space=pltpu.VMEM)
    hbm = pl.BlockSpec(memory_space=pltpu.HBM)
    feat = jax.ShapeDtypeStruct((tokens, width), BF16)
    proj = jax.ShapeDtypeStruct((DS, width), F32)

    def buf(*shape, dtype=BF16):
        return pltpu.VMEM(shape, dtype)

    feats = functools.partial(buf, tokens, width)
    out = pl.pallas_call(
        functools.partial(kernel, (NDP, NSEQ, NHEAD, HL, HDIM, Q)),
        out_shape=[jax.ShapeDtypeStruct((tokens, DH), BF16)] + [feat] * 6 + [proj] * 2,
        in_specs=[hbm] * 3 + [pl.BlockSpec(memory_space=pltpu.SMEM)] + [hbm] * 6,
        out_specs=[vmem] * 9,
        scratch_shapes=[
            feats(), feats(), feats(),
            buf(Z, Y, Q, width),
            buf(Y, Z, Q, width),
            buf(NHEAD, tokens, DH),
            feats(), feats(), feats(),
            buf(HL, tokens, tokens, dtype=F32),
            buf(HL, tokens, tokens, dtype=F32),
            feats(), feats(), feats(),
            feats(dtype=F32), feats(dtype=F32),
            feats(), feats(), feats(), feats(), feats(),
            buf(Z, Y, Q, width),
            buf(Y, Z, Q, width),
            buf(2, Z // 2, Y, Q, width),
            buf(2, Y // 2, Z, Q, width),
            buf(Y - 1, Q, width),
            buf(Z - 1, Q, width),
            buf(2, NDP, Q, width),
            buf(X, tokens, DH),
            buf(X, tokens, DH),
            buf(X, tokens, DH, dtype=F32),
            buf(X - 1, tokens, DH),
            buf(X - 1, tokens, DH),
            pltpu.SemaphoreType.DMA((SEMS,)),
        ],
        compiler_params=pltpu.CompilerParams(
            collective_id=0, has_side_effects=True, vmem_limit_bytes=24 * 1024 * 1024
        ),
    )(*held[:3], mask, *held[3:])
    out = [pltpu.with_memory_space_constraint(o, pltpu.VMEM) for o in out]
    out = pl.pallas_call(
        store,
        out_shape=[jax.ShapeDtypeStruct(o.shape, o.dtype) for o in out],
        in_specs=[vmem] * 9,
        out_specs=[hbm] * 9,
        scratch_shapes=[pltpu.SemaphoreType.DMA((9,))],
    )(*out)
    return tuple(o[None, None] for o in out[:7]) + (out[7].T, out[8].T)


def solution(mesh):
    tokens = P("dp", "seq", None, "head")
    weights = P("head", "seq")
    dims = tuple(mesh.shape[a] for a in ("dp", "seq", "head"))
    return jax.shard_map(
        functools.partial(per_device, dims),
        mesh=mesh,
        in_specs=(tokens,) * 3 + (P("dp", "seq", "head", None, None),) + (tokens,) * 3 + (weights,) * 2 + (tokens,),
        out_specs=(tokens,) * 7 + (weights,) * 2,
        check_vma=False,
    )
```

```python
import functools
import math

import jax
import jax.numpy as jnp
from jax import lax
from jax.experimental import pallas as pl
from jax.experimental.pallas import tpu as pltpu
from jax.sharding import PartitionSpec as P

MESH = pl.DeviceIdType.MESH
BF16 = jnp.bfloat16
F32 = jnp.float32
NEG = -1e30
ORDER = (
    "w1", "sf", "tf", "wz2", "wy2", "c", "wz3", "wy3", "cd", "ps", "pt", "rz1", "ry1", "wz4", "wy4", "rz2", "ry2",
    "rz3", "ry3", "gt", "wzf", "u1", "rz4", "ry4", "sa", "ta", "tb", "u2", "ss", "ts", "gs", "sb", "ud",
)
SEMS = 192


def dot(a, b):
    return lax.dot_general(a, b, (((1,), (0,)), ((), ())), preferred_element_type=F32)


def dot_nt(a, b):
    return lax.dot_general(a, b, (((1,), (1,)), ((), ())), preferred_element_type=F32)


def dot_tn(a, b):
    return lax.dot_general(a, b, (((0,), (0,)), ((), ())), preferred_element_type=F32)


def wait_for(view, sem):
    pltpu.make_async_copy(view, view, sem).wait()


def kernel(
    dims,
    sq_in, sk_in, sv_in, mask, tq, tk, tv, sp, tp, cot,
    upd, gsq, gsk, gsv, gtq, gtk, gtv, gsp, gtp,
    sq, sk, sv, wts, wtt, cotb, tqb, tkb, tvb,
    s_shares, t_shares, s_att, t_att, t_att_tok, gs_acc, gt_acc, g_t, g_tok, q_g, k_g, v_g,
    ps, pt, rs_s, rs_t, sec_s, sec_t, fin,
    u_out, u_in, u_keep, u_send, u_recv,
    sems,
):
    NDP, NSEQ, NHEAD, HL, HDIM, Q = dims
    Z, Y, X = NSEQ // 2, NDP * 2, NHEAD // 2
    TOK, LW = sq.shape
    DS = NDP * Q
    TB = TOK // NSEQ
    DH = cot.shape[1]
    scale = 1.0 / math.sqrt(HDIM)

    dp = lax.axis_index("dp")
    seq = lax.axis_index("seq")
    head = lax.axis_index("head")
    z, yh = seq // 2, lax.rem(seq, 2)
    y = yh * NDP + dp
    x, core = head // 2, lax.rem(head, 2)

    def at_y(place):
        return {"dp": lax.rem(place, NDP), "seq": z * 2 + place // NDP}

    def at_z(place):
        return {"seq": place * 2 + yh}

    def at_x(place):
        return {"head": place * 2 + core}

    sibling = {"head": x * 2 + 1 - core}
    counter = iter(range(SEMS))

    def sem(part):
        return sems.at[next(counter)]

    def local(src, dst, done):
        pltpu.make_async_copy(src, dst, done).start()

    def send(src, dst, send_sem, recv_sem, to):
        pltpu.make_async_remote_copy(
            src_ref=src, dst_ref=dst, send_sem=send_sem, recv_sem=recv_sem,
            device_id=to, device_id_type=MESH,
        ).start()

    barrier = pltpu.get_barrier_semaphore()

    def greet(to):
        pl.semaphore_signal(barrier, inc=1, device_id=to, device_id_type=MESH)

    @pl.loop(1, NSEQ)
    def _(i):
        greet({"seq": lax.rem(seq + i, NSEQ)})

    @pl.loop(1, NDP)
    def _(i):
        other = lax.rem(dp + i, NDP)
        greet({"dp": other, "seq": z * 2})
        greet({"dp": other, "seq": z * 2 + 1})

    @pl.loop(1, X)
    def _(i):
        greet(at_x(lax.rem(x + i, X)))

    greet(sibling)

    spatial = ((sq_in, sq), (sk_in, sk), (sv_in, sv))
    spatial_l = [sem("in") for _ in spatial]
    for (src, dst), l in zip(spatial, spatial_l):
        local(src, dst, l)
    own_l, cot_l = [sem("in") for _ in range(2)], sem("in")
    own_s = wts.at[z, pl.ds(yh * NDP, NDP)]
    local(sp, own_s, own_l[0])
    local(tp.at[dp], wtt.at[y, 1], own_l[1])
    local(cot, cotb.at[head], cot_l)

    pl.semaphore_wait(barrier, NSEQ - 1 + 2 * (NDP - 1) + X)

    def all_to_all(src, dst, send_sem, recv_sem):
        mine = pl.ds(pl.multiple_of(seq * TB, TB), TB)

        @pl.loop(1, NSEQ)
        def _(i):
            other = lax.rem(seq + i, NSEQ)
            send(
                src.at[pl.ds(pl.multiple_of(other * TB, TB), TB)], dst.at[mine],
                send_sem, recv_sem, {"seq": other},
            )

    def rest(ref):
        return ref.at[pl.ds(0, (NSEQ - 1) * TB)]

    mine = pl.ds(pl.multiple_of(seq * TB, TB), TB)
    qkv = ((tq, tqb), (tk, tkb), (tv, tvb))
    qkv_s, qkv_r, qkv_l = [[sem("qkv") for _ in qkv] for _ in range(3)]
    for (src, dst), s, r, l in zip(qkv, qkv_s, qkv_r, qkv_l):
        all_to_all(src, dst, s, r)
        local(src.at[mine], dst.at[mine], l)

    def spatial_piece(chunk, piece):
        return wts.at[chunk, pl.ds((yh if piece == 0 else 1 - yh) * NDP, NDP)]

    def temporal_piece(chunk, piece):
        return wtt.at[chunk, pl.ds(piece * (Z // 2), Z // 2)]

    zq_s, zq_r = sem("w"), [sem("w"), sem("w")]
    for i in range(1, Z):
        slot = (1 - i) % Z
        send(tp.at[dp], wtt.at[y, slot], zq_s, zq_r[slot // (Z // 2)], at_z(lax.rem(z + i, Z)))

    mir_s, mir_r = sem("w"), sem("w")
    send(sp, own_s, mir_s, mir_r, {"dp": NDP - 1 - dp, "seq": z * 2 + 1 - yh})

    class Ring:
        def __init__(self, part, n, me, where):
            self.n, self.me = n, me
            self.to = where(lax.rem(me + 1, n)), where(lax.rem(me + n - 1, n))
            self.sems = {
                (way, piece): [(sem(part), sem(part)) for _ in range(self.hops(way, piece))]
                for way in range(2) for piece in range(2)
            }

        def hops(self, way, piece):
            return self.n // 2 if way == piece else self.n // 2 - 1

        def place(self, way, k):
            return lax.rem(self.me + (k if way == 0 else -k) + self.n, self.n)

    class Gather(Ring):
        def __init__(self, part, n, me, where, view):
            super().__init__(part, n, me, where)
            self.view = view

        def arrived(self, way, piece, j):
            wait_for(self.view(self.place(way, -j), piece), self.sems[way, piece][j - 1][1])

        def hop(self, piece, j):
            for way in range(2):
                if j <= self.hops(way, piece):
                    if j > 1:
                        self.arrived(way, piece, j - 1)
                    v = self.view(self.place(way, 1 - j), piece)
                    send(v, v, *self.sems[way, piece][j - 1], self.to[way])

        def finish(self):
            for piece in range(2):
                for way in range(2):
                    self.arrived(way, piece, self.hops(way, piece))

        def drain(self):
            for (way, piece), pairs in self.sems.items():
                for s, _ in pairs:
                    wait_for(self.view(self.me, piece), s)

    wz = Gather("w", Z, z, at_z, spatial_piece)
    wy = Gather("w", Y, y, at_y, temporal_piece)
    wait_for(own_s, own_l[0])
    wz.hop(0, 1)

    cot_s = [sem("cot") for _ in range(X)]
    cot_r = [sem("cot") for _ in range(X - 1)]
    cot_sib = sem("cot")
    for i in range(1, X):
        send(cot, cotb.at[head], cot_s[i - 1], cot_r[i - 1], at_x(lax.rem(x + i, X)))
    send(cot, cotb.at[head], cot_s[X - 1], cot_sib, sibling)

    def heads(ref, h):
        return ref[:, h * HDIM : (h + 1) * HDIM]

    def forward(h, q, k, v, bias, shares):
        scores = dot_nt(heads(q, h), heads(k, h)) * scale + bias
        e = jnp.exp(scores - jnp.max(scores, axis=-1, keepdims=True))
        part = e * (1.0 / jnp.sum(e, axis=-1, keepdims=True))
        shares[h] = part
        return dot(part.astype(BF16), heads(v, h)).astype(BF16)

    def backward(h, q, k, v, g, shares):
        share = shares[h]
        weight = share.astype(BF16)
        grad = heads(g, h)
        grad_shares = dot_nt(grad, heads(v, h))
        centre = jnp.sum(share * grad_shares, axis=-1, keepdims=True)
        grad_scores = (share * (grad_shares - centre)).astype(BF16)
        dq = (dot(grad_scores, heads(k, h)) * scale).astype(BF16)
        dk = (dot_tn(grad_scores, heads(q, h)) * scale).astype(BF16)
        dv = dot_tn(weight, grad).astype(BF16)
        return dq, dk, dv

    class Scatter(Ring):
        def __init__(self, part, n, me, where, buf, landing):
            super().__init__(part, n, me, where)
            self.buf, self.landing = buf, landing
            size = buf.shape[1] // 2
            self.rows = [pl.ds(0, size), pl.ds(size, size)]

        def landed(self, way, piece, j):
            return self.landing.at[way, j - 1, self.rows[piece]]

        def hop(self, piece, j):
            for way in range(2):
                hops = self.hops(way, piece)
                if j <= hops:
                    dest = self.place(way, hops + 1 - j)
                    if j > 1:
                        came = self.landed(way, piece, j - 1)
                        wait_for(came, self.sems[way, piece][j - 2][1])
                        total = self.buf[dest, self.rows[piece]].astype(F32) + came[...].astype(F32)
                        self.buf[dest, self.rows[piece]] = total.astype(BF16)
                    send(
                        self.buf.at[dest, self.rows[piece]], self.landed(way, piece, j),
                        *self.sems[way, piece][j - 1], self.to[way],
                    )

        def finish(self, piece):
            total = self.buf[self.me, self.rows[piece]].astype(F32)
            for way in range(2):
                hops = self.hops(way, piece)
                came = self.landed(way, piece, hops)
                wait_for(came, self.sems[way, piece][hops - 1][1])
                total = total + came[...].astype(F32)
            self.buf[self.me, self.rows[piece]] = total.astype(BF16)

        def drain(self):
            for (way, piece), pairs in self.sems.items():
                for s, _ in pairs:
                    wait_for(self.buf.at[self.me, self.rows[piece]], s)

    rz = Scatter("p", Z, z, at_z, ps, rs_s)
    ry = Scatter("p", Y, y, at_y, pt, rs_t)

    def block_t(b):
        return wtt[:, pl.ds(lax.rem(b - z + 1 + Z, Z), 1)].reshape(DH, LW)

    def block_s(b):
        return wts[b].reshape(DH, LW)

    def update(b):
        return dot_nt(s_att[...], block_s(b)) + dot_nt(t_att[...], block_t(b))

    rows = lax.broadcasted_iota(jnp.int32, (TOK, TOK), 0)
    cols = lax.broadcasted_iota(jnp.int32, (TOK, TOK), 1)
    ta_s, ta_r, gt_s, gt_r = sem("ta"), sem("ta"), sem("gt"), sem("gt")
    fwd_s, fwd_r = [[sem("cot") for _ in range(X - 1)] for _ in range(2)]
    us_s, us_r, ux_s, ux_r = [sem("u") for _ in range(4)]
    grads = ((q_g, gtq), (k_g, gtk), (v_g, gtv))
    grads_s, grads_r = [[sem("grads") for _ in grads] for _ in range(2)]
    sec_ss, sec_sr, sec_ts, sec_tr = [sem("sec") for _ in range(4)]
    fin_ss, fin_sr, fin_ts, fin_tr = [sem("fin") for _ in range(4)]

    def spatial_forward():
        for (src, dst), l in zip(spatial, spatial_l):
            wait_for(dst, l)
        NB = mask.shape[-1]
        tile = TOK // NB
        for h in range(HL):
            bias = jnp.zeros((TOK, TOK), F32)
            for a in range(NB):
                for b in range(NB):
                    value = (mask[0, 0, h, a, b].astype(F32) - 1.0) * -NEG
                    inside = jnp.logical_and(rows // tile == a, cols // tile == b)
                    bias = jnp.where(inside, value, bias)
            s_att[:, h * HDIM : (h + 1) * HDIM] = forward(h, sq, sk, sv, bias, s_shares)

    def weights_start():
        wait_for(own_s, mir_r)
        wz.hop(1, 1)
        wait_for(wtt.at[y, 1], own_l[1])
        wait_for(wtt.at[y, pl.ds(0, Z // 2 - 1)], zq_r[0])
        wy.hop(0, 1)
        wait_for(wtt.at[y, pl.ds(0, Z // 2)], zq_r[1])
        wy.hop(1, 1)

    def temporal_forward():
        for (src, dst), r, l in zip(qkv, qkv_r, qkv_l):
            wait_for(rest(dst), r)
            wait_for(dst.at[mine], l)
        same = jnp.where(lax.rem(rows, TB) == lax.rem(cols, TB), 0.0, NEG).astype(F32)
        for h in range(HL):
            t_att_tok[:, h * HDIM : (h + 1) * HDIM] = forward(h, tqb, tkb, tvb, same, t_shares)
        all_to_all(t_att_tok, t_att, ta_s, ta_r)
        t_att[mine] = t_att_tok[mine]

    def cotangent_on():
        for i in range(1, X):
            slot = cotb.at[lax.rem(x + X - i, X) * 2 + core]
            wait_for(slot, cot_r[i - 1])
            send(slot, slot, fwd_s[i - 1], fwd_r[i - 1], sibling)

    def cotangent_done():
        wait_for(cotb.at[head], cot_l)
        wait_for(cotb.at[head], cot_sib)
        for i in range(1, X):
            wait_for(cotb.at[head], fwd_r[i - 1])

    def spatial_product():
        @pl.loop(0, Z)
        def _(b):
            ps[b] = dot_tn(cotb[b], s_att[...]).astype(BF16).reshape(Y, Q, LW)

    def temporal_product():
        wait_for(rest(t_att), ta_r)

        @pl.loop(0, Z)
        def _(b):
            pt[:, pl.ds(b, 1)] = dot_tn(cotb[b], t_att[...]).astype(BF16).reshape(Y, 1, Q, LW)

    def temporal_gradient():
        wy.finish()
        gt_acc[...] = jnp.zeros_like(gt_acc)

        @pl.loop(0, Z)
        def _(b):
            gt_acc[...] += dot(cotb[b], block_t(b))

        g_t[...] = gt_acc[...].astype(BF16)
        all_to_all(g_t, g_tok, gt_s, gt_r)
        g_tok[mine] = g_t[mine]

    def spatial_gradient():
        gs_acc[...] = jnp.zeros_like(gs_acc)

        @pl.loop(0, Z)
        def _(b):
            gs_acc[...] += dot(cotb[b], block_s(b))

    def update_other():
        @pl.loop(0, X)
        def _(i):
            u_out[i] = update(i * 2 + 1 - core).astype(BF16)
            send(u_out.at[i], u_in.at[i], us_s, us_r, sibling)

    def update_own():
        @pl.loop(0, X)
        def _(i):
            u_keep[i] = update(i * 2 + core)

        wait_for(u_in, us_r)

        @pl.loop(1, X)
        def _(i):
            other = lax.rem(x + i, X)
            u_send[i - 1] = (u_keep[other] + u_in[other].astype(F32)).astype(BF16)
            send(u_send.at[i - 1], u_recv.at[i - 1], ux_s, ux_r, at_x(other))

    def update_done():
        wait_for(u_recv, ux_r)
        total = u_keep[x] + u_in[x].astype(F32)
        for i in range(X - 1):
            total = total + u_recv[i].astype(F32)
        upd[...] = total.astype(BF16)

    def temporal_backward():
        wait_for(rest(g_tok), gt_r)
        for h in range(HL):
            f = slice(h * HDIM, (h + 1) * HDIM)
            q_g[:, f], k_g[:, f], v_g[:, f] = backward(h, tqb, tkb, tvb, g_tok, t_shares)
        for (src, dst), s, r in zip(grads, grads_s, grads_r):
            all_to_all(src, dst, s, r)
            dst[mine] = src[mine]

    def spatial_backward():
        g_s = gs_acc[...].astype(BF16)
        for h in range(HL):
            f = slice(h * HDIM, (h + 1) * HDIM)
            gsq[:, f], gsk[:, f], gsv[:, f] = backward(h, sq, sk, sv, g_s, s_shares)

    def across(ring, buf, mine, me, n, landing, left, came, where):
        for piece in range(2):
            ring.finish(piece)

            @pl.loop(piece * (n // 2), (piece + 1) * (n // 2))
            def _(other):
                @pl.when(other != me)
                def _():
                    slot = lax.rem(other - me + n, n) - 1
                    send(buf.at[mine, other], landing.at[slot], left, came, where(other))

    def spatial_across():
        across(rz, ps, z, y, Y, sec_s, sec_ss, sec_sr, at_y)

    def temporal_across():
        across(ry, pt, y, z, Z, sec_t, sec_ts, sec_tr, at_z)

    def share(own, parts, count, slot, left, came):
        total = own.astype(F32)
        for i in range(count - 1):
            total = total + parts[i].astype(F32)
        fin[slot, dp] = (total * (1.0 / NDP)).astype(BF16)

        @pl.loop(1, NDP)
        def _(i):
            send(fin.at[slot, dp], fin.at[slot, dp], left, came, {"dp": lax.rem(dp + i, NDP)})

    def spatial_share():
        wait_for(sec_s, sec_sr)
        share(ps[z, y], sec_s, Y, 0, fin_ss, fin_sr)

    def temporal_share():
        wait_for(sec_t, sec_tr)
        share(pt[y, z], sec_t, Z, 1, fin_ts, fin_tr)

    steps = {
        "sf": spatial_forward, "w1": weights_start, "tf": temporal_forward, "c": cotangent_on, "cd": cotangent_done,
        "ps": spatial_product, "pt": temporal_product, "gt": temporal_gradient, "gs": spatial_gradient,
        "wzf": wz.finish, "u1": update_other, "u2": update_own, "ud": update_done, "tb": temporal_backward,
        "sb": spatial_backward, "sa": spatial_across, "ta": temporal_across, "ss": spatial_share, "ts": temporal_share,
    }
    rings = {"wz": wz, "wy": wy, "rz": rz, "ry": ry}
    for name in ORDER:
        if name in steps:
            steps[name]()
        else:
            for piece in range(2):
                rings[name[:2]].hop(piece, int(name[2:]))
    for (src, dst), r in zip(grads, grads_r):
        wait_for(rest(dst), r)

    for (src, dst), s in zip(qkv, qkv_s):
        wait_for(rest(dst), s)
    wait_for(own_s, mir_s)
    wait_for(wtt.at[y, pl.ds(0, Z - 1)], zq_s)
    for s in cot_s + fwd_s:
        wait_for(cotb.at[head], s)
    wz.drain()
    wy.drain()
    rz.drain()
    ry.drain()
    for s in (ta_s, gt_s):
        wait_for(rest(t_att), s)
    for s in grads_s:
        wait_for(rest(t_att), s)
    wait_for(u_in, us_s)
    wait_for(u_recv, ux_s)
    wait_for(sec_s, sec_ss)
    wait_for(sec_t, sec_ts)
    for slot, left, came, out in ((0, fin_ss, fin_sr, gsp), (1, fin_ts, fin_tr, gtp)):
        wait_for(fin.at[slot, pl.ds(0, NDP - 1)], came)
        wait_for(fin.at[slot, pl.ds(0, NDP - 1)], left)
        out[...] = fin[slot].reshape(DS, LW).astype(F32)


def store(*refs):
    count = len(refs) // 2
    sems = refs[-1]
    copies = [pltpu.make_async_copy(refs[i], refs[count + i], sems.at[i]) for i in range(count)]
    for copy in copies:
        copy.start()
    for copy in copies:
        copy.wait()


def per_device(dims, *args):
    NDP, NSEQ, NHEAD = dims
    sq, sk, sv, mask, tq, tk, tv, sp, tp, cot = args
    tokens, width = sq.shape[2:]
    HL = mask.shape[2]
    HDIM = width // HL
    DS, DH = sp.shape[1], cot.shape[3]
    Z, Y, X = NSEQ // 2, NDP * 2, NHEAD // 2
    Q = DS // NDP
    flat = [a.reshape(a.shape[2:]) for a in (sq, sk, sv, tq, tk, tv, cot)]
    held = flat[:6] + [p.T.reshape(NDP, Q, width) for p in (sp, tp)] + flat[6:]
    mask = pltpu.with_memory_space_constraint(mask, pltpu.HBM)
    held = [pltpu.with_memory_space_constraint(a, pltpu.HBM) for a in held]
    vmem = pl.BlockSpec(memory_space=pltpu.VMEM)
    hbm = pl.BlockSpec(memory_space=pltpu.HBM)
    feat = jax.ShapeDtypeStruct((tokens, width), BF16)
    proj = jax.ShapeDtypeStruct((DS, width), F32)

    def buf(*shape, dtype=BF16):
        return pltpu.VMEM(shape, dtype)

    feats = functools.partial(buf, tokens, width)
    out = pl.pallas_call(
        functools.partial(kernel, (NDP, NSEQ, NHEAD, HL, HDIM, Q)),
        out_shape=[jax.ShapeDtypeStruct((tokens, DH), BF16)] + [feat] * 6 + [proj] * 2,
        in_specs=[hbm] * 3 + [pl.BlockSpec(memory_space=pltpu.SMEM)] + [hbm] * 6,
        out_specs=[vmem] * 9,
        scratch_shapes=[
            feats(), feats(), feats(),
            buf(Z, Y, Q, width),
            buf(Y, Z, Q, width),
            buf(NHEAD, tokens, DH),
            feats(), feats(), feats(),
            buf(HL, tokens, tokens, dtype=F32),
            buf(HL, tokens, tokens, dtype=F32),
            feats(), feats(), feats(),
            feats(dtype=F32), feats(dtype=F32),
            feats(), feats(), feats(), feats(), feats(),
            buf(Z, Y, Q, width),
            buf(Y, Z, Q, width),
            buf(2, Z // 2, Y, Q, width),
            buf(2, Y // 2, Z, Q, width),
            buf(Y - 1, Q, width),
            buf(Z - 1, Q, width),
            buf(2, NDP, Q, width),
            buf(X, tokens, DH),
            buf(X, tokens, DH),
            buf(X, tokens, DH, dtype=F32),
            buf(X - 1, tokens, DH),
            buf(X - 1, tokens, DH),
            pltpu.SemaphoreType.DMA((SEMS,)),
        ],
        compiler_params=pltpu.CompilerParams(
            collective_id=0, has_side_effects=True, vmem_limit_bytes=24 * 1024 * 1024
        ),
    )(*held[:3], mask, *held[3:])
    out = [pltpu.with_memory_space_constraint(o, pltpu.VMEM) for o in out]
    out = pl.pallas_call(
        store,
        out_shape=[jax.ShapeDtypeStruct(o.shape, o.dtype) for o in out],
        in_specs=[vmem] * 9,
        out_specs=[hbm] * 9,
        scratch_shapes=[pltpu.SemaphoreType.DMA((9,))],
    )(*out)
    return tuple(o[None, None] for o in out[:7]) + (out[7].T, out[8].T)


def solution(mesh):
    tokens = P("dp", "seq", None, "head")
    weights = P("head", "seq")
    dims = tuple(mesh.shape[a] for a in ("dp", "seq", "head"))
    return jax.shard_map(
        functools.partial(per_device, dims),
        mesh=mesh,
        in_specs=(tokens,) * 3 + (P("dp", "seq", "head", None, None),) + (tokens,) * 3 + (weights,) * 2 + (tokens,),
        out_specs=(tokens,) * 7 + (weights,) * 2,
        check_vma=False,
    )
```
